32 devices in a mesh: expert: 16 (over z, y, x), seq: 2 (over core).
Axes of the slice: x: 2, y: 2, z: 4, core: 2. Of those that a mesh axis runs over, the one named last changes fastest.
Arguments:
- hidden_rows: bfloat16 [2048, 8, 1024], P(('expert', 'seq')), may hold values from -16 to 16
- routes: int32 [2048, 8], P(('expert', 'seq')), may hold values from 0 to 15, all different within a row; in each aligned block of 64 rows (0 to 63, 64 to 127, ...) at most 64 rows name the same one
- down_weight: bfloat16 [16, 7168, 1024], P('expert', 'seq'), may hold values from -0.1875 to 0.1875
- probe: bfloat16 [7168, 256], P('seq'), may hold values from -0.0625 to 0.0625
Outputs:
- basis: float32 [7168, 256], P(('seq', 'expert'))
- coefficients: float32 [16, 256, 1024], P('expert', None, 'seq')
The draws below stay inside these ranges and needn't reach their ends.
Inputs may be any that keep to these rules, and one draw needn't show every extreme that they name: `routes`: in each aligned block of 64 tokens no expert is named in more than 64 places, and some expert in exactly 64; the 8 experts of a token differ.
All inputs are finite; a program needn't handle non-finite values.
Results may differ from the reference program's by a relative error of at most 0.0054.
Values may be sent and summed in bfloat16 or wider, within the bound.
A program may use at most 64 MiB of HBM per device.

```python
import math
import jax
import jax.numpy as jnp
import numpy as np
from jax import lax

D = 7168
FF = 1024
TOP = 8
P_SIZE = 256
TOK_DEV = 64
EXPERTS = 16
TOKENS = 2048
CAP = 64
ROW_MEAN = 1024


def draw_hidden_rows(key, part):
    key = jax.random.fold_in(key, 7)
    base_key, column_key, row_key = jax.random.split(key, 3)
    column_scale = jnp.exp(jax.random.uniform(column_key, (FF,), jnp.float32, math.log(0.3), math.log(3.0)))
    row_scale = jnp.exp(jax.random.uniform(row_key, (TOKENS, TOP, 1), jnp.float32, math.log(0.5), math.log(2.0)))
    values = jax.random.normal(base_key, (TOKENS, TOP, FF), jnp.float32)
    return jnp.clip(values * column_scale * row_scale, -16.0, 16.0).astype(jnp.bfloat16)


def shard_levels(key, shape, pieces, low, high):
    gain, own = 1.0, jax.random.fold_in(key, 6)
    for axis_at, blocks in pieces:
        draws = jnp.exp(jax.random.uniform(jax.random.fold_in(own, axis_at), (blocks,), jnp.float32, low / len(pieces), high / len(pieces)))
        gain = gain * jnp.repeat(draws, shape[axis_at] // blocks).reshape([-1 if axis == axis_at else 1 for axis in range(len(shape))])
    return gain


def shared_out(rng, own, number, rows, amount, top, bound, skew):
    order = jax.random.permutation(rng, amount)
    heavy_load, ordinary = load_shares(amount, rows * top, bound, skew, True), load_shares(amount, rows * top, bound, skew, False)
    places = jnp.arange(amount)

    def named(lengths, turn):
        used = int((lengths > 0).sum())
        fixed = max(1, used // 4)
        passed = fixed + (places - fixed + turn * (used - fixed)) % max(1, amount - fixed)
        return jnp.zeros((amount,), jnp.int32).at[order[jnp.where(places < fixed, places, passed)]].set(jnp.asarray(lengths, jnp.int32))

    lengths = jnp.where(number % 4 == 0, named(heavy_load, number // 4), named(ordinary, number - number // 4 - 1))
    mixed = jax.random.permutation(jax.random.fold_in(own, 3), amount)
    giver, taker = mixed[0:amount // 2 * 2:2], mixed[1:amount // 2 * 2:2]
    slack = jnp.minimum(lengths[giver] - 1, bound - lengths[taker]) // 2
    slack = jnp.where((giver == order[0]) | (taker == order[0]) | (lengths[taker] == 0), 0, jnp.maximum(slack, 0))
    passed = jax.random.randint(jax.random.fold_in(own, 4), (amount // 2,), 0, 1 << 20) % (slack + 1)
    lengths = lengths.at[giver].add(-passed).at[taker].add(passed)
    members = jnp.searchsorted(jnp.cumsum(lengths), jnp.arange(rows * top), side="right").astype(jnp.int32)
    table = members.reshape(top, rows).T
    table = table[jax.random.permutation(jax.random.fold_in(own, 1), rows)]
    turn = jax.random.randint(jax.random.fold_in(own, 2), (rows, 1), 0, top)
    return jnp.take_along_axis(table, (jnp.arange(top)[None, :] + turn) % top, axis=1)


def load_shares(count, total, bound, lean, full):
    portions = [(1 << 20) // math.isqrt(rank ** lean) + 1 for rank in range(1, count + 1)]
    largest = bound if full else min(bound, max(-(-total // count), total * portions[0] // sum(portions)))
    least = 1 if total - largest >= count - 1 else 0
    given, spare = [largest] + [least] * (count - 1), total - largest - least * (count - 1)
    while spare > 0:
        free = [i for i in range(1, count) if given[i] < largest] or [i for i in range(1, count) if given[i] < bound]
        pool, remaining = sum([portions[i] for i in free]), spare
        for i in free:
            extra = min(bound - given[i], max(1, remaining * portions[i] // pool), spare)
            given[i] = given[i] + extra
            spare = spare - extra
    return np.array(given)


def noise(stream_key, shape, width, limit, cuts=(), held_as=jnp.bfloat16):
    drawn = width * jax.random.normal(stream_key, shape, jnp.float32)
    if cuts:
        drawn = drawn * shard_levels(stream_key, shape, cuts, -0.22, 0.18)
    return jnp.clip(drawn, -limit, limit).astype(held_as)


def setup_inputs(seed: int = 0) -> dict:
    key_list = jax.random.split(jax.random.key(seed), 5)
    hidden_rows = draw_hidden_rows(jax.random.fold_in(key_list[4], 71), 0)
    routes_keys = jax.random.split(jax.random.fold_in(key_list[1], 1), TOKENS // TOK_DEV)
    routes_turns = jax.random.permutation(jax.random.fold_in(key_list[1], 3), TOKENS // TOK_DEV)
    routes = jax.vmap(lambda own, number: shared_out(jax.random.fold_in(key_list[1], 2), own, number, TOK_DEV, EXPERTS, TOP, CAP, 2))(routes_keys, routes_turns).reshape((TOKENS, TOP))
    down_weight = noise(key_list[2], (EXPERTS, D, FF), FF ** -0.5, 0.1875, ((0, 16), (1, 2)))
    probe = noise(key_list[3], (D, P_SIZE), D ** -0.5, 0.0625, ((0, 2),))
    return {"hidden_rows": hidden_rows, "routes": routes, "down_weight": down_weight, "probe": probe}


def reference(hidden_rows, routes, down_weight, probe):
    flat_rows = hidden_rows.reshape(-1, FF)
    expert_ids = routes.reshape(-1).astype(jnp.int32)
    row_limit = (TOKENS // TOK_DEV) * CAP
    row_order = jnp.argsort(expert_ids, stable=True).astype(jnp.int32)
    row_order = jnp.concatenate([row_order, jnp.zeros((row_limit,), jnp.int32)])
    labels = jnp.arange(EXPERTS, dtype=jnp.int32)
    counts = jnp.sum((expert_ids[:, None] == labels[None, :]).astype(jnp.int32), axis=0).astype(jnp.int32)
    starts = (jnp.cumsum(counts) - counts).astype(jnp.int32)

    def expert_panel(running, inputs):
        weight, first, count = inputs
        probe_proj = lax.dot_general(weight, probe, (((0,), (0,)), ((), ())), preferred_element_type=jnp.float32).astype(jnp.bfloat16)
        picked = lax.dynamic_slice(row_order, (first.astype(jnp.int32),), (row_limit,))
        live_mask = jnp.arange(row_limit, dtype=jnp.int32) < count
        chosen_rows = jnp.where(live_mask[:, None], flat_rows[picked], jnp.zeros((), jnp.bfloat16))
        mixed = jnp.dot(chosen_rows, probe_proj, preferred_element_type=jnp.float32).astype(jnp.bfloat16)
        gram_full = lax.dot_general(chosen_rows, mixed, (((0,), (0,)), ((), ())), preferred_element_type=jnp.float32) / ROW_MEAN
        panel_image = jnp.dot(weight, gram_full.astype(jnp.bfloat16), preferred_element_type=jnp.float32)
        return running + panel_image, None

    basis, _ = lax.scan(expert_panel, jnp.zeros((D, P_SIZE), jnp.float32), (down_weight, starts, counts))
    basis_bf = basis.astype(jnp.bfloat16)

    def coefficient_block(weight):
        return lax.dot_general(basis_bf, weight, (((0,), (0,)), ((), ())), preferred_element_type=jnp.float32)

    coefficients = lax.map(coefficient_block, down_weight)
    return (basis, coefficients)
```

```python
import functools

import jax
import jax.numpy as jnp
from jax import lax
from jax.experimental import pallas as pl
from jax.experimental.pallas import tpu as pltpu
from jax.sharding import PartitionSpec as P

MESH = pl.DeviceIdType.MESH
F32 = jnp.float32
BF16 = jnp.bfloat16


def contract0(a, b):
    return lax.dot_general(a, b, (((0,), (0,)), ((), ())), preferred_element_type=F32)


def panel_kernel(
    row_mean, w, gram, basis_out, coef_out,
    g_recv, g_bf, sa1, sb1, ra1, rb1, pa2, pb2, p3, sa2, sb2, ra2, rb2, s3, r3, gath, coef, c_recv,
    g_sem, a1_sem, b1_sem, a2_sem, b2_sem, z_sem, gz_sem, ga1_sem, gb1_sem, ga2_sem, gb2_sem, c_sem,
):
    e, s = lax.axis_index("expert"), lax.axis_index("seq")
    x, y, z = e % 2, (e // 2) % 2, e // 4
    to_x = {"expert": e + 1 - 2 * x}
    to_y = {"expert": e + 2 - 4 * y}
    to_core = {"seq": 1 - s}
    to_z = lambda d: {"expert": ((z + d) % 4) * 4 + e % 4}
    rows, half = basis_out.shape[0], basis_out.shape[1] // 2

    def chunk(zz, yr, xr):
        return zz * 4 + ((y + yr) % 2) * 2 + (x + xr) % 2

    def w_rows(c):
        return w[pl.ds(pl.multiple_of(c * rows, rows), rows), :]

    def remote(src, dst, sem, at, where):
        return pltpu.make_async_remote_copy(
            src_ref=src, dst_ref=dst, send_sem=sem.at[(0, *at)], recv_sem=sem.at[(1, *at)],
            device_id=where, device_id_type=MESH,
        )

    barrier = pltpu.get_barrier_semaphore()
    for where in (to_x, to_y, to_core, to_z(1), to_z(2), to_z(3)):
        pl.semaphore_signal(barrier, inc=1, device_id=where, device_id_type=MESH)
    pl.semaphore_wait(barrier, 6)

    swap = remote(gram, g_recv, g_sem, (), to_core)
    swap.start()
    swap.wait()
    g_bf[...] = ((gram[...] + g_recv[...]) / row_mean).astype(BF16)

    def panel(d, yr, xr):
        return jnp.dot(w_rows(chunk((z + d) % 4, yr, xr)), g_bf[...], preferred_element_type=F32)

    copy_a1 = lambda yr, d: remote(sa1.at[yr, d], ra1.at[yr, d], a1_sem, (yr, d), to_x)
    copy_b1 = lambda xr, d: remote(sb1.at[xr, d], rb1.at[xr, d], b1_sem, (xr, d), to_y)
    copy_a2 = lambda d: remote(sa2.at[d], ra2.at[d], a2_sem, (d,), to_y)
    copy_b2 = lambda d: remote(sb2.at[d], rb2.at[d], b2_sem, (d,), to_x)
    copy_z = lambda d: remote(s3.at[d], r3.at[d], z_sem, (d,), to_z(d))

    def over_z(step):
        lax.fori_loop(0, 4, lambda i, carry: (step((i + 1) % 4), carry)[1], 0)

    def both_far(d):
        value = panel(d, 1, 1)
        sa1[1, d] = value[:, :half].astype(BF16)
        copy_a1(1, d).start()
        sb1[1, d] = value[:, half:].astype(BF16)
        copy_b1(1, d).start()

    def one_far(d):
        value = panel(d, 0, 1)
        sa1[0, d] = value[:, :half].astype(BF16)
        copy_a1(0, d).start()
        pb2[d] = value[:, half:]
        value = panel(d, 1, 0)
        sb1[0, d] = value[:, half:].astype(BF16)
        copy_b1(0, d).start()
        pa2[d] = value[:, :half]

    def near(d):
        p3[d] = panel(d, 0, 0)

    def second(d):
        copy_a1(1, d).wait_recv()
        sa2[d] = (pa2[d] + ra1[1, d].astype(F32)).astype(BF16)
        copy_a2(d).start()
        copy_b1(1, d).wait_recv()
        sb2[d] = (pb2[d] + rb1[1, d].astype(F32)).astype(BF16)
        copy_b2(d).start()

    def third(d):
        copy_a1(0, d).wait_recv()
        copy_a2(d).wait_recv()
        first = p3[d, :, :half] + ra1[0, d].astype(F32) + ra2[d].astype(F32)
        copy_b1(0, d).wait_recv()
        copy_b2(d).wait_recv()
        last = p3[d, :, half:] + rb1[0, d].astype(F32) + rb2[d].astype(F32)
        return first, last

    def third_send(i, carry):
        d = i + 1
        first, last = third(d)
        s3[d, 0] = first.astype(BF16)
        s3[d, 1] = last.astype(BF16)
        copy_z(d).start()
        return carry

    over_z(both_far)
    over_z(one_far)
    over_z(near)
    over_z(second)
    lax.fori_loop(0, 3, third_send, 0)
    first, last = third(0)
    for d in (1, 2, 3):
        copy_z(d).wait_recv()
        first += r3[d, 0].astype(F32)
        last += r3[d, 1].astype(F32)
    basis_out[:, :half] = first
    basis_out[:, half:] = last
    gath[e, 0] = first.astype(BF16)
    gath[e, 1] = last.astype(BF16)

    def held(d, yr, xr):
        return chunk((z + 4 - d) % 4, yr, xr)

    def pass_on(c, part, sem, at, where):
        return remote(gath.at[c, part], gath.at[c, part], sem, at, where)

    copy_gz = lambda d: remote(gath.at[e], gath.at[e], gz_sem, (d,), to_z(d))
    copy_ga1 = lambda d: pass_on(held(d, 0, 0), 0, ga1_sem, (d,), to_y)
    copy_gb1 = lambda d: pass_on(held(d, 0, 0), 1, gb1_sem, (d,), to_x)
    copy_ga2 = lambda yr, d: pass_on(held(d, yr, 0), 0, ga2_sem, (yr, d), to_x)
    copy_gb2 = lambda xr, d: pass_on(held(d, 0, xr), 1, gb2_sem, (xr, d), to_y)

    def came_z(d):
        c = held(d, 0, 0)
        return remote(gath.at[c], gath.at[c], gz_sem, (d,), to_z(d))

    def came_a1(d):
        return pass_on(held(d, 1, 0), 0, ga1_sem, (d,), to_y)

    def came_b1(d):
        return pass_on(held(d, 0, 1), 1, gb1_sem, (d,), to_x)

    def came_a2(yr, d):
        return pass_on(held(d, yr, 1), 0, ga2_sem, (yr, d), to_x)

    def came_b2(xr, d):
        return pass_on(held(d, 1, xr), 1, gb2_sem, (xr, d), to_y)

    for d in (2, 1, 3):
        copy_gz(d).start()
    coef[...] = jnp.zeros_like(coef)

    def add_coef(c):
        block = jnp.concatenate([gath[c, 0], gath[c, 1]], axis=1)
        value = contract0(block, w_rows(c))
        width = value.shape[1] // 2
        coef[0] += value[:, :width]
        coef[1] += value[:, width:]

    def hand_out(d):
        copy_ga1(d).start()
        copy_gb1(d).start()
        copy_ga2(0, d).start()
        copy_gb2(0, d).start()

    hand_out(0)

    def from_z(i, carry):
        came_z(i + 1).wait_recv()
        hand_out(i + 1)
        return carry

    lax.fori_loop(0, 3, from_z, 0)

    def forward(d, carry):
        came_a1(d).wait_recv()
        copy_ga2(1, d).start()
        came_b1(d).wait_recv()
        copy_gb2(1, d).start()
        add_coef(held(d, 0, 0))
        return carry

    lax.fori_loop(0, 4, forward, 0)

    def take_near(d, carry):
        came_b2(0, d).wait_recv()
        add_coef(held(d, 1, 0))
        came_a2(0, d).wait_recv()
        add_coef(held(d, 0, 1))
        return carry

    lax.fori_loop(0, 4, take_near, 0)

    def take_far(d, carry):
        came_a2(1, d).wait_recv()
        came_b2(1, d).wait_recv()
        add_coef(held(d, 1, 1))
        return carry

    lax.fori_loop(0, 4, take_far, 0)

    share = remote(coef.at[1 - s], c_recv, c_sem, (), to_core)
    share.start()

    def drain(d, carry):
        for k in (0, 1):
            copy_a1(k, d).wait_send()
            copy_b1(k, d).wait_send()
            copy_ga2(k, d).wait_send()
            copy_gb2(k, d).wait_send()
        copy_a2(d).wait_send()
        copy_b2(d).wait_send()
        copy_ga1(d).wait_send()
        copy_gb1(d).wait_send()
        return carry

    lax.fori_loop(0, 4, drain, 0)
    for d in (1, 2, 3):
        copy_z(d).wait_send()
        copy_gz(d).wait_send()
    share.wait()
    coef_out[...] = coef[s] + c_recv[...]


def panel_call(weight, gram_part, row_mean):
    depth, width = weight.shape
    cols = gram_part.shape[1]
    rows, half = depth // 16, cols // 2
    dma = pltpu.SemaphoreType.DMA
    vmem = pltpu.VMEM
    return pl.pallas_call(
        functools.partial(panel_kernel, row_mean),
        out_shape=(
            jax.ShapeDtypeStruct((rows, cols), F32),
            jax.ShapeDtypeStruct((cols, width // 2), F32),
        ),
        in_specs=[pl.BlockSpec(memory_space=vmem)] * 2,
        out_specs=[pl.BlockSpec(memory_space=vmem)] * 2,
        scratch_shapes=[
            vmem((width, cols), F32),
            vmem((width, cols), BF16),
            vmem((2, 4, rows, half), BF16),
            vmem((2, 4, rows, half), BF16),
            vmem((2, 4, rows, half), BF16),
            vmem((2, 4, rows, half), BF16),
            vmem((4, rows, half), F32),
            vmem((4, rows, half), F32),
            vmem((4, rows, cols), F32),
            vmem((4, rows, half), BF16),
            vmem((4, rows, half), BF16),
            vmem((4, rows, half), BF16),
            vmem((4, rows, half), BF16),
            vmem((4, 2, rows, half), BF16),
            vmem((4, 2, rows, half), BF16),
            vmem((16, 2, rows, half), BF16),
            vmem((2, cols, width // 2), F32),
            vmem((cols, width // 2), F32),
            dma((2,)),
            dma((2, 2, 4)),
            dma((2, 2, 4)),
            dma((2, 4)),
            dma((2, 4)),
            dma((2, 4)),
            dma((2, 4)),
            dma((2, 4)),
            dma((2, 4)),
            dma((2, 2, 4)),
            dma((2, 2, 4)),
            dma((2,)),
        ],
        compiler_params=pltpu.CompilerParams(
            collective_id=0, has_side_effects=True, vmem_limit_bytes=40 * 2**20
        ),
        cost_estimate=pl.CostEstimate(
            flops=4 * depth * width * cols, bytes_accessed=2 * depth * width, transcendentals=0
        ),
    )(weight, gram_part)


def body(hidden_rows, routes, down_weight, probe):
    weight = down_weight[0]
    tok_count, top_count = routes.shape
    feature_width = hidden_rows.shape[2]
    experts = lax.axis_size("expert")
    capacity = 2 * tok_count * top_count // experts
    row_mean = tok_count * top_count * lax.axis_size("seq")
    partial_value = lax.dot_general(
        weight, probe, (((0,), (0,)), ((), ())), preferred_element_type=jnp.float32
    )
    probe_proj = lax.psum(partial_value, "seq").astype(jnp.bfloat16)
    expert_ids = routes.reshape(-1)
    onehot = (expert_ids[:, None] == jnp.arange(experts, dtype=jnp.int32)[None, :]).astype(
        jnp.int32
    )
    position = jnp.sum(onehot * (jnp.cumsum(onehot, axis=0) - 1), axis=1)
    destination = expert_ids * capacity + position
    outgoing = jnp.zeros((experts * capacity, feature_width), jnp.bfloat16)
    outgoing = outgoing.at[destination].set(hidden_rows.reshape(-1, feature_width))
    outgoing = outgoing.reshape(experts, capacity, feature_width)
    arrived = lax.all_to_all(outgoing, "expert", split_axis=0, concat_axis=0, tiled=True)
    arrived_rows = arrived.reshape(-1, feature_width)
    mixed = jnp.dot(arrived_rows, probe_proj, preferred_element_type=jnp.float32).astype(
        jnp.bfloat16
    )
    gram_part = lax.dot_general(
        arrived_rows, mixed, (((0,), (0,)), ((), ())), preferred_element_type=jnp.float32
    )
    if experts == 16 and lax.axis_size("seq") == 2:
        basis_rows, coefficients = panel_call(weight, gram_part, row_mean)
        return (basis_rows, coefficients[None])
    gram_full = lax.psum(gram_part, "seq") / row_mean
    panel_image = jnp.dot(
        weight, gram_full.astype(jnp.bfloat16), preferred_element_type=jnp.float32
    )
    basis_rows = lax.psum_scatter(panel_image, "expert", scatter_dimension=0, tiled=True)
    coef_part = lax.dot_general(
        lax.all_gather(basis_rows.astype(jnp.bfloat16), "expert", axis=0, tiled=True),
        weight,
        (((0,), (0,)), ((), ())),
        preferred_element_type=jnp.float32,
    )
    coefficients = lax.psum_scatter(coef_part, "seq", scatter_dimension=1, tiled=True)
    return (basis_rows, coefficients[None])


def solution(mesh):
    in_specs = (
        P(("expert", "seq"), None, None),
        P(("expert", "seq"), None),
        P("expert", "seq", None),
        P("seq", None),
    )
    out_specs = (P(("seq", "expert"), None), P("expert", None, "seq"))
    return jax.shard_map(body, mesh=mesh, in_specs=in_specs, out_specs=out_specs, check_vma=False)
```

```python
import functools

import jax
import jax.numpy as jnp
from jax import lax
from jax.experimental import pallas as pl
from jax.experimental.pallas import tpu as pltpu
from jax.sharding import PartitionSpec as P

MESH = pl.DeviceIdType.MESH
F32 = jnp.float32
BF16 = jnp.bfloat16


def contract0(a, b):
    return lax.dot_general(a, b, (((0,), (0,)), ((), ())), preferred_element_type=F32)


def contract1(a, b):
    return lax.dot_general(a, b, (((1,), (1,)), ((), ())), preferred_element_type=F32)


def panel_kernel(
    row_mean, w_any, probe_any, ids, tokens, basis_out, coef_out,
    w, probe, sent, arr, p_part, p_recv, pt, gt, gr, sp, rp, g_bf, sa1, sb1, ra1, rb1, pa2, pb2, p3, sa2, sb2, ra2, rb2, s3, r3, gath, coef, c_recv,
    load_sem, rows_sem, p_sem, px_sem, pf_sem, gs_sem, gx_sem, gf_sem, a1_sem, b1_sem, a2_sem, b2_sem, z_sem, gz_sem, ga1_sem, gb1_sem, ga2_sem, gb2_sem, c_sem,
):
    e, s = lax.axis_index("expert"), lax.axis_index("seq")
    x, y, z = e % 2, (e // 2) % 2, e // 4
    to_x = {"expert": e + 1 - 2 * x}
    to_y = {"expert": e + 2 - 4 * y}
    to_core = {"seq": 1 - s}
    to_z = lambda d: {"expert": ((z + d) % 4) * 4 + e % 4}
    rows, half = basis_out.shape[0], basis_out.shape[1] // 2

    def chunk(zz, yr, xr):
        return zz * 4 + ((y + yr) % 2) * 2 + (x + xr) % 2

    def w_rows(c):
        return w[pl.ds(pl.multiple_of(c * rows, rows), rows), :]

    def remote(src, dst, sem, at, where):
        return pltpu.make_async_remote_copy(
            src_ref=src, dst_ref=dst, send_sem=sem.at[(0, *at)], recv_sem=sem.at[(1, *at)],
            device_id=where, device_id_type=MESH,
        )

    cap = tokens.shape[0] // 8
    own_half = z // 2
    partner = {"expert": (e + 8) % 16}

    def near_chip(q):
        return own_half * 8 + (z + q // 4) % 2 * 4 + (y + q // 2) % 2 * 2 + (x + q) % 2

    load_w = pltpu.make_async_copy(w_any, w, load_sem.at[0])
    load_probe = pltpu.make_async_copy(probe_any, probe, load_sem.at[1])
    load_w.start()
    load_probe.start()

    barrier = pltpu.get_barrier_semaphore()
    for q in range(1, 8):
        pl.semaphore_signal(
            barrier, inc=1, device_id={"expert": near_chip(q)}, device_id_type=MESH
        )
    far = [{"expert": (2 - 2 * own_half + k) * 4 + e % 4} for k in (0, 1)]
    for where in (to_core, *far):
        pl.semaphore_signal(barrier, inc=1, device_id=where, device_id_type=MESH)

    amount = tokens.shape[0]
    names = ids[...]
    mark = (lax.broadcasted_iota(jnp.int32, (16, amount), 0) == names).astype(F32)
    before = (
        lax.broadcasted_iota(jnp.int32, (amount, amount), 0)
        < lax.broadcasted_iota(jnp.int32, (amount, amount), 1)
    ).astype(F32).astype(BF16)
    rank = jnp.dot(mark.astype(BF16), before, preferred_element_type=F32)
    place = jnp.sum(mark * rank, axis=0, keepdims=True).astype(jnp.int32) + names * cap

    copy_rows = lambda k, q: remote(
        sent.at[k, q], arr.at[k, q], rows_sem, (k, q), {"expert": near_chip(q)}
    )

    def block_for(q):
        chip = near_chip(q)
        line = lax.broadcasted_iota(jnp.int32, (2 * cap, amount), 0)
        wanted = jnp.where(line < cap, chip * cap + line, ((chip + 8) % 16 - 1) * cap + line)
        pick = (wanted == place).astype(F32).astype(BF16)
        return jnp.dot(pick, tokens[...], preferred_element_type=F32).astype(BF16)

    pl.semaphore_wait(barrier, 10)

    def send_rows(i, carry):
        q = 7 - i
        block = block_for(q)
        sent[0, q] = block[:cap]
        copy_rows(0, q).start()
        sent[1, q] = block[cap:]
        copy_rows(1, q).start()
        return carry

    lax.fori_loop(0, 7, send_rows, 0)
    block = block_for(0)
    arr[0, 0] = block[:cap]
    arr[1, 0] = block[cap:]

    load_probe.wait()
    load_w.wait()
    p_part[...] = jnp.zeros_like(p_part)
    part = 256

    def project(i, carry):
        at = pl.ds(pl.multiple_of(i * part, part), part)
        p_part[...] += contract0(probe[at, :], w[at, :])
        return carry

    lax.fori_loop(0, w.shape[0] // part, project, 0)
    swap = remote(p_part, p_recv, p_sem, (), to_core)
    swap.start()
    swap.wait()
    pt[0] = (p_part[...] + p_recv[...]).astype(BF16).reshape(pt.shape[1:])
    across = remote(pt.at[0, s], pt.at[1, s], px_sem, (), partner)
    across.start()

    def gram_of(k, first):
        rows_k = arr[k, first:first + 4].reshape(4 * cap, arr.shape[3])
        proj = pt[k].reshape(2 * pt.shape[2], pt.shape[3])
        mixed = contract1(rows_k, proj).astype(BF16)
        return contract0(mixed, rows_k).reshape(gt.shape[1:])

    for q in (3, 2, 1):
        copy_rows(0, q).wait_recv()
    gt[0] = gram_of(0, 0)
    across.wait_recv()
    hand = remote(pt.at[1, s], pt.at[1, s], pf_sem, (), to_core)
    hand.start()
    for q in (3, 2, 1):
        copy_rows(1, q).wait_recv()
    remote(pt.at[1, 1 - s], pt.at[1, 1 - s], pf_sem, (), to_core).wait_recv()
    gt[1] = gram_of(1, 0)
    for q in (7, 6, 5, 4):
        copy_rows(1, q).wait_recv()
    gt[1] += gram_of(1, 4)
    copy_gs = lambda k: remote(gt.at[k, 1 - s], gr.at[k], gs_sem, (k,), to_core)
    copy_gs(1).start()
    for q in (7, 6, 5, 4):
        copy_rows(0, q).wait_recv()
    gt[0] += gram_of(0, 4)
    copy_gs(0).start()
    copy_gs(1).wait_recv()
    sp[...] = (gt[1, s] + gr[1]).astype(BF16)
    cross = remote(sp, rp, gx_sem, (), partner)
    cross.start()
    copy_gs(0).wait_recv()
    cross.wait_recv()
    g_bf[s] = ((gt[0, s] + gr[0] + rp[...].astype(F32)) / row_mean).astype(BF16)
    spread = remote(g_bf.at[s], g_bf.at[s], gf_sem, (), to_core)
    spread.start()
    remote(g_bf.at[1 - s], g_bf.at[1 - s], gf_sem, (), to_core).wait_recv()

    def panel(d, yr, xr):
        g_all = g_bf[...].reshape(2 * half, g_bf.shape[2])
        return contract1(w_rows(chunk((z + d) % 4, yr, xr)), g_all)

    copy_a1 = lambda yr, d: remote(sa1.at[yr, d], ra1.at[yr, d], a1_sem, (yr, d), to_x)
    copy_b1 = lambda xr, d: remote(sb1.at[xr, d], rb1.at[xr, d], b1_sem, (xr, d), to_y)
    copy_a2 = lambda d: remote(sa2.at[d], ra2.at[d], a2_sem, (d,), to_y)
    copy_b2 = lambda d: remote(sb2.at[d], rb2.at[d], b2_sem, (d,), to_x)
    copy_z = lambda d: remote(s3.at[d], r3.at[d], z_sem, (d,), to_z(d))

    def over_z(step):
        lax.fori_loop(0, 4, lambda i, carry: (step((i + 1) % 4), carry)[1], 0)

    def both_far(d):
        value = panel(d, 1, 1)
        sa1[1, d] = value[:, :half].astype(BF16)
        copy_a1(1, d).start()
        sb1[1, d] = value[:, half:].astype(BF16)
        copy_b1(1, d).start()

    def one_far(d):
        value = panel(d, 0, 1)
        sa1[0, d] = value[:, :half].astype(BF16)
        copy_a1(0, d).start()
        pb2[d] = value[:, half:]
        value = panel(d, 1, 0)
        sb1[0, d] = value[:, half:].astype(BF16)
        copy_b1(0, d).start()
        pa2[d] = value[:, :half]

    def near(d):
        p3[d] = panel(d, 0, 0)

    def second(d):
        copy_a1(1, d).wait_recv()
        sa2[d] = (pa2[d] + ra1[1, d].astype(F32)).astype(BF16)
        copy_a2(d).start()
        copy_b1(1, d).wait_recv()
        sb2[d] = (pb2[d] + rb1[1, d].astype(F32)).astype(BF16)
        copy_b2(d).start()

    def third(d):
        copy_a1(0, d).wait_recv()
        copy_a2(d).wait_recv()
        first = p3[d, :, :half] + ra1[0, d].astype(F32) + ra2[d].astype(F32)
        copy_b1(0, d).wait_recv()
        copy_b2(d).wait_recv()
        last = p3[d, :, half:] + rb1[0, d].astype(F32) + rb2[d].astype(F32)
        return first, last

    def third_send(i, carry):
        d = i + 1
        first, last = third(d)
        s3[d, 0] = first.astype(BF16)
        s3[d, 1] = last.astype(BF16)
        copy_z(d).start()
        return carry

    over_z(both_far)
    over_z(one_far)
    over_z(near)
    over_z(second)
    lax.fori_loop(0, 3, third_send, 0)
    first, last = third(0)
    for d in (1, 2, 3):
        copy_z(d).wait_recv()
        first += r3[d, 0].astype(F32)
        last += r3[d, 1].astype(F32)
    basis_out[:, :half] = first
    basis_out[:, half:] = last
    gath[e, 0] = first.astype(BF16)
    gath[e, 1] = last.astype(BF16)

    def held(d, yr, xr):
        return chunk((z + 4 - d) % 4, yr, xr)

    def pass_on(c, part, sem, at, where):
        return remote(gath.at[c, part], gath.at[c, part], sem, at, where)

    copy_gz = lambda d: remote(gath.at[e], gath.at[e], gz_sem, (d,), to_z(d))
    copy_ga1 = lambda d: pass_on(held(d, 0, 0), 0, ga1_sem, (d,), to_y)
    copy_gb1 = lambda d: pass_on(held(d, 0, 0), 1, gb1_sem, (d,), to_x)
    copy_ga2 = lambda yr, d: pass_on(held(d, yr, 0), 0, ga2_sem, (yr, d), to_x)
    copy_gb2 = lambda xr, d: pass_on(held(d, 0, xr), 1, gb2_sem, (xr, d), to_y)

    def came_z(d):
        c = held(d, 0, 0)
        return remote(gath.at[c], gath.at[c], gz_sem, (d,), to_z(d))

    def came_a1(d):
        return pass_on(held(d, 1, 0), 0, ga1_sem, (d,), to_y)

    def came_b1(d):
        return pass_on(held(d, 0, 1), 1, gb1_sem, (d,), to_x)

    def came_a2(yr, d):
        return pass_on(held(d, yr, 1), 0, ga2_sem, (yr, d), to_x)

    def came_b2(xr, d):
        return pass_on(held(d, 1, xr), 1, gb2_sem, (xr, d), to_y)

    for d in (2, 1, 3):
        copy_gz(d).start()
    coef[...] = jnp.zeros_like(coef)

    def add_coef(c):
        block = jnp.concatenate([gath[c, 0], gath[c, 1]], axis=1)
        value = contract0(block, w_rows(c))
        width = value.shape[1] // 2
        coef[0] += value[:, :width]
        coef[1] += value[:, width:]

    def hand_out(d):
        copy_ga1(d).start()
        copy_gb1(d).start()
        copy_ga2(0, d).start()
        copy_gb2(0, d).start()

    hand_out(0)

    def forward(d):
        came_a1(d).wait_recv()
        copy_ga2(1, d).start()
        came_b1(d).wait_recv()
        copy_gb2(1, d).start()
        add_coef(held(d, 0, 0))

    def from_z(i, carry):
        came_z(i + 1).wait_recv()
        hand_out(i + 1)
        forward(i)
        return carry

    lax.fori_loop(0, 3, from_z, 0)
    forward(3)

    def take_near(d, carry):
        came_b2(0, d).wait_recv()
        add_coef(held(d, 1, 0))
        came_a2(0, d).wait_recv()
        add_coef(held(d, 0, 1))
        return carry

    lax.fori_loop(0, 4, take_near, 0)

    def take_far(d, carry):
        came_a2(1, d).wait_recv()
        came_b2(1, d).wait_recv()
        add_coef(held(d, 1, 1))
        return carry

    lax.fori_loop(0, 4, take_far, 0)

    share = remote(coef.at[1 - s], c_recv, c_sem, (), to_core)
    share.start()

    def drain(d, carry):
        for k in (0, 1):
            copy_a1(k, d).wait_send()
            copy_b1(k, d).wait_send()
            copy_ga2(k, d).wait_send()
            copy_gb2(k, d).wait_send()
        copy_a2(d).wait_send()
        copy_b2(d).wait_send()
        copy_ga1(d).wait_send()
        copy_gb1(d).wait_send()
        return carry

    lax.fori_loop(0, 4, drain, 0)
    for d in (1, 2, 3):
        copy_z(d).wait_send()
        copy_gz(d).wait_send()
    for q in range(1, 8):
        copy_rows(0, q).wait_send()
        copy_rows(1, q).wait_send()
    for copy in (across, hand, copy_gs(0), copy_gs(1), cross, spread):
        copy.wait_send()
    share.wait()
    coef_out[...] = coef[s] + c_recv[...]


def panel_call(weight, probe, ids, tokens, row_mean):
    depth, width = weight.shape
    cols = probe.shape[1]
    cap = tokens.shape[0] // 8
    rows, half = depth // 16, cols // 2
    dma = pltpu.SemaphoreType.DMA
    vmem = pltpu.VMEM
    return pl.pallas_call(
        functools.partial(panel_kernel, row_mean),
        out_shape=(
            jax.ShapeDtypeStruct((rows, cols), F32),
            jax.ShapeDtypeStruct((cols, width // 2), F32),
        ),
        in_specs=[pl.BlockSpec(memory_space=pl.ANY)] * 2 + [pl.BlockSpec(memory_space=vmem)] * 2,
        out_specs=[pl.BlockSpec(memory_space=vmem)] * 2,
        scratch_shapes=[
            vmem((depth, width), BF16),
            vmem((depth, cols), BF16),
            vmem((2, 8, cap, width), BF16),
            vmem((2, 8, cap, width), BF16),
            vmem((cols, width), F32),
            vmem((cols, width), F32),
            vmem((2, 2, half, width), BF16),
            vmem((2, 2, half, width), F32),
            vmem((2, half, width), F32),
            vmem((half, width), BF16),
            vmem((half, width), BF16),
            vmem((2, half, width), BF16),
            vmem((2, 4, rows, half), BF16),
            vmem((2, 4, rows, half), BF16),
            vmem((2, 4, rows, half), BF16),
            vmem((2, 4, rows, half), BF16),
            vmem((4, rows, half), F32),
            vmem((4, rows, half), F32),
            vmem((4, rows, cols), F32),
            vmem((4, rows, half), BF16),
            vmem((4, rows, half), BF16),
            vmem((4, rows, half), BF16),
            vmem((4, rows, half), BF16),
            vmem((4, 2, rows, half), BF16),
            vmem((4, 2, rows, half), BF16),
            vmem((16, 2, rows, half), BF16),
            vmem((2, cols, width // 2), F32),
            vmem((cols, width // 2), F32),
            dma((2,)),
            dma((2, 2, 8)),
            dma((2,)),
            dma((2,)),
            dma((2,)),
            dma((2, 2)),
            dma((2,)),
            dma((2,)),
            dma((2, 2, 4)),
            dma((2, 2, 4)),
            dma((2, 4)),
            dma((2, 4)),
            dma((2, 4)),
            dma((2, 4)),
            dma((2, 4)),
            dma((2, 4)),
            dma((2, 2, 4)),
            dma((2, 2, 4)),
            dma((2,)),
        ],
        compiler_params=pltpu.CompilerParams(
            collective_id=0, has_side_effects=True, vmem_limit_bytes=52 * 2**20
        ),
        cost_estimate=pl.CostEstimate(
            flops=8 * depth * width * cols, bytes_accessed=2 * depth * width, transcendentals=0
        ),
    )(weight, probe, ids, tokens)


def body(hidden_rows, routes, down_weight, probe):
    weight = down_weight[0]
    tok_count, top_count = routes.shape
    feature_width = hidden_rows.shape[2]
    experts = lax.axis_size("expert")
    capacity = 2 * tok_count * top_count // experts
    row_mean = tok_count * top_count * lax.axis_size("seq")
    if experts == 16 and lax.axis_size("seq") == 2:
        ids = routes.reshape(1, -1)
        tokens = hidden_rows.reshape(-1, feature_width)
        basis_rows, coefficients = panel_call(weight, probe, ids, tokens, row_mean)
        return (basis_rows, coefficients[None])
    partial_value = lax.dot_general(
        weight, probe, (((0,), (0,)), ((), ())), preferred_element_type=jnp.float32
    )
    probe_proj = lax.psum(partial_value, "seq").astype(jnp.bfloat16)
    expert_ids = routes.reshape(-1)
    onehot = (expert_ids[:, None] == jnp.arange(experts, dtype=jnp.int32)[None, :]).astype(
        jnp.int32
    )
    position = jnp.sum(onehot * (jnp.cumsum(onehot, axis=0) - 1), axis=1)
    destination = expert_ids * capacity + position
    outgoing = jnp.zeros((experts * capacity, feature_width), jnp.bfloat16)
    outgoing = outgoing.at[destination].set(hidden_rows.reshape(-1, feature_width))
    outgoing = outgoing.reshape(experts, capacity, feature_width)
    arrived = lax.all_to_all(outgoing, "expert", split_axis=0, concat_axis=0, tiled=True)
    arrived_rows = arrived.reshape(-1, feature_width)
    mixed = jnp.dot(arrived_rows, probe_proj, preferred_element_type=jnp.float32).astype(
        jnp.bfloat16
    )
    gram_part = lax.dot_general(
        arrived_rows, mixed, (((0,), (0,)), ((), ())), preferred_element_type=jnp.float32
    )
    gram_full = lax.psum(gram_part, "seq") / row_mean
    panel_image = jnp.dot(
        weight, gram_full.astype(jnp.bfloat16), preferred_element_type=jnp.float32
    )
    basis_rows = lax.psum_scatter(panel_image, "expert", scatter_dimension=0, tiled=True)
    coef_part = lax.dot_general(
        lax.all_gather(basis_rows.astype(jnp.bfloat16), "expert", axis=0, tiled=True),
        weight,
        (((0,), (0,)), ((), ())),
        preferred_element_type=jnp.float32,
    )
    coefficients = lax.psum_scatter(coef_part, "seq", scatter_dimension=1, tiled=True)
    return (basis_rows, coefficients[None])


def solution(mesh):
    in_specs = (
        P(("expert", "seq"), None, None),
        P(("expert", "seq"), None),
        P("expert", "seq", None),
        P("seq", None),
    )
    out_specs = (P(("seq", "expert"), None), P("expert", None, "seq"))
    return jax.shard_map(body, mesh=mesh, in_specs=in_specs, out_specs=out_specs, check_vma=False)
```

```python
import functools

import jax
import jax.numpy as jnp
from jax import lax
from jax.experimental import pallas as pl
from jax.experimental.pallas import tpu as pltpu
from jax.sharding import PartitionSpec as P

MESH = pl.DeviceIdType.MESH
F32 = jnp.float32
BF16 = jnp.bfloat16


def contract0(a, b):
    return lax.dot_general(a, b, (((0,), (0,)), ((), ())), preferred_element_type=F32)


def contract1(a, b):
    return lax.dot_general(a, b, (((1,), (1,)), ((), ())), preferred_element_type=F32)


def panel_kernel(
    row_mean, w_any, probe_any, tokens_any, ids, basis_out, coef_out,
    tokens, w, probe, sent, arr, p_part, p_recv, pt, gt, gr, sp, rp, g_bf, sa1, sb1, ra1, rb1, pa2, pb2, p3, sa2, sb2, ra2, rb2, s3, r3, gath, coef, c_recv,
    load_sem, rows_sem, p_sem, px_sem, pf_sem, gs_sem, gx_sem, gf_sem, a1_sem, b1_sem, a2_sem, b2_sem, z_sem, gz_sem, ga1_sem, gb1_sem, ga2_sem, gb2_sem, c_sem,
):
    e, s = lax.axis_index("expert"), lax.axis_index("seq")
    x, y, z = e % 2, (e // 2) % 2, e // 4
    to_x = {"expert": e + 1 - 2 * x}
    to_y = {"expert": e + 2 - 4 * y}
    to_core = {"seq": 1 - s}

    def z_of(k):
        return (z // 2 + k // 2) % 2 * 2 + (z + k) % 2

    def to_z(k):
        return {"expert": z_of(k) * 4 + e % 4}

    rows, half = basis_out.shape[0], basis_out.shape[1] // 2

    def chunk(zz, yr, xr):
        return zz * 4 + ((y + yr) % 2) * 2 + (x + xr) % 2

    def w_rows(c):
        return w[pl.ds(pl.multiple_of(c * rows, rows), rows), :]

    def remote(src, dst, sem, at, where):
        return pltpu.make_async_remote_copy(
            src_ref=src, dst_ref=dst, send_sem=sem.at[(0, *at)], recv_sem=sem.at[(1, *at)],
            device_id=where, device_id_type=MESH,
        )

    cap = tokens.shape[0] // 8
    own_half = z // 2
    partner = {"expert": (e + 8) % 16}

    def near_chip(q):
        return own_half * 8 + (z + q // 4) % 2 * 4 + (y + q // 2) % 2 * 2 + (x + q) % 2

    load_w = pltpu.make_async_copy(w_any, w, load_sem.at[0])
    load_probe = pltpu.make_async_copy(probe_any, probe, load_sem.at[1])
    load_tokens = pltpu.make_async_copy(tokens_any, tokens, load_sem.at[2])
    load_tokens.start()
    load_w.start()
    load_probe.start()

    barrier = pltpu.get_barrier_semaphore()
    for q in range(1, 8):
        pl.semaphore_signal(
            barrier, inc=1, device_id={"expert": near_chip(q)}, device_id_type=MESH
        )
    far = [{"expert": (2 - 2 * own_half + k) * 4 + e % 4} for k in (0, 1)]
    for where in (to_core, *far):
        pl.semaphore_signal(barrier, inc=1, device_id=where, device_id_type=MESH)

    amount = tokens.shape[0]
    names = ids[...]
    mark = (lax.broadcasted_iota(jnp.int32, (16, amount), 0) == names).astype(F32)
    before = (
        lax.broadcasted_iota(jnp.int32, (amount, amount), 0)
        < lax.broadcasted_iota(jnp.int32, (amount, amount), 1)
    ).astype(F32).astype(BF16)
    rank = jnp.dot(mark.astype(BF16), before, preferred_element_type=F32)
    place = jnp.sum(mark * rank, axis=0, keepdims=True).astype(jnp.int32) + names * cap

    def slot_chip(i):
        return near_chip(5 * i % 8)

    copy_rows = lambda k, i: remote(
        sent.at[k, i], arr.at[k, i], rows_sem, (k, i), {"expert": slot_chip(i)}
    )

    def block_for(i):
        chip = slot_chip(i)
        line = lax.broadcasted_iota(jnp.int32, (2 * cap, amount), 0)
        wanted = jnp.where(line < cap, chip * cap + line, ((chip + 8) % 16 - 1) * cap + line)
        pick = (wanted == place).astype(F32).astype(BF16)
        return jnp.dot(pick, tokens[...], preferred_element_type=F32).astype(BF16)

    load_tokens.wait()
    pl.semaphore_wait(barrier, 10)

    def send_rows(j, carry):
        i = j + 1
        block = block_for(i)
        sent[0, i] = block[:cap]
        copy_rows(0, i).start()
        sent[1, i] = block[cap:]
        copy_rows(1, i).start()
        return carry

    lax.fori_loop(0, 7, send_rows, 0)
    block = block_for(0)
    arr[0, 0] = block[:cap]
    arr[1, 0] = block[cap:]

    load_probe.wait()
    load_w.wait()
    p_part[...] = jnp.zeros_like(p_part)
    part = 256

    def project(i, carry):
        at = pl.ds(pl.multiple_of(i * part, part), part)
        p_part[...] += contract0(probe[at, :], w[at, :])
        return carry

    lax.fori_loop(0, w.shape[0] // part, project, 0)
    swap = remote(p_part, p_recv, p_sem, (), to_core)
    swap.start()
    swap.wait()
    pt[0] = (p_part[...] + p_recv[...]).astype(BF16).reshape(pt.shape[1:])
    across = remote(pt.at[0, s], pt.at[1, s], px_sem, (), partner)
    across.start()

    def gram_of(k, first):
        rows_k = arr[k, first:first + 4].reshape(4 * cap, arr.shape[3])
        proj = pt[k].reshape(2 * pt.shape[2], pt.shape[3])
        mixed = contract1(rows_k, proj).astype(BF16)
        return contract0(mixed, rows_k).reshape(gt.shape[1:])

    for q in (1, 2, 3):
        copy_rows(0, q).wait_recv()
    gt[0] = gram_of(0, 0)
    across.wait_recv()
    hand = remote(pt.at[1, s], pt.at[1, s], pf_sem, (), to_core)
    hand.start()
    for q in (1, 2, 3):
        copy_rows(1, q).wait_recv()
    remote(pt.at[1, 1 - s], pt.at[1, 1 - s], pf_sem, (), to_core).wait_recv()
    gt[1] = gram_of(1, 0)
    for q in (4, 5, 6, 7):
        copy_rows(1, q).wait_recv()
    gt[1] += gram_of(1, 4)
    copy_gs = lambda k: remote(gt.at[k, 1 - s], gr.at[k], gs_sem, (k,), to_core)
    copy_gs(1).start()
    for q in (4, 5, 6, 7):
        copy_rows(0, q).wait_recv()
    gt[0] += gram_of(0, 4)
    copy_gs(0).start()
    copy_gs(1).wait_recv()
    sp[...] = (gt[1, s] + gr[1]).astype(BF16)
    cross = remote(sp, rp, gx_sem, (), partner)
    cross.start()
    copy_gs(0).wait_recv()
    cross.wait_recv()
    g_bf[s] = ((gt[0, s] + gr[0] + rp[...].astype(F32)) / row_mean).astype(BF16)
    spread = remote(g_bf.at[s], g_bf.at[s], gf_sem, (), to_core)
    spread.start()
    remote(g_bf.at[1 - s], g_bf.at[1 - s], gf_sem, (), to_core).wait_recv()

    def panel(d, yr, xr):
        g_all = g_bf[...].reshape(2 * half, g_bf.shape[2])
        return contract1(w_rows(chunk(z_of(d), yr, xr)), g_all)

    copy_a1 = lambda yr, d: remote(sa1.at[yr, d], ra1.at[yr, d], a1_sem, (yr, d), to_x)
    copy_b1 = lambda xr, d: remote(sb1.at[xr, d], rb1.at[xr, d], b1_sem, (xr, d), to_y)
    copy_a2 = lambda d: remote(sa2.at[d], ra2.at[d], a2_sem, (d,), to_y)
    copy_b2 = lambda d: remote(sb2.at[d], rb2.at[d], b2_sem, (d,), to_x)
    copy_z = lambda d: remote(s3.at[d], r3.at[d], z_sem, (d,), to_z(d))

    def both_far(d):
        value = panel(d, 1, 1)
        sa1[1, d] = value[:, :half].astype(BF16)
        copy_a1(1, d).start()
        sb1[1, d] = value[:, half:].astype(BF16)
        copy_b1(1, d).start()

    def one_far(d):
        value = panel(d, 0, 1)
        sa1[0, d] = value[:, :half].astype(BF16)
        copy_a1(0, d).start()
        pb2[d] = value[:, half:]
        value = panel(d, 1, 0)
        sb1[0, d] = value[:, half:].astype(BF16)
        copy_b1(0, d).start()
        pa2[d] = value[:, :half]

    def near(d):
        p3[d] = panel(d, 0, 0)

    def second(d):
        copy_a1(1, d).wait_recv()
        sa2[d] = (pa2[d] + ra1[1, d].astype(F32)).astype(BF16)
        copy_a2(d).start()
        copy_b1(1, d).wait_recv()
        sb2[d] = (pb2[d] + rb1[1, d].astype(F32)).astype(BF16)
        copy_b2(d).start()

    def third(d):
        copy_a1(0, d).wait_recv()
        copy_a2(d).wait_recv()
        first = p3[d, :, :half] + ra1[0, d].astype(F32) + ra2[d].astype(F32)
        copy_b1(0, d).wait_recv()
        copy_b2(d).wait_recv()
        last = p3[d, :, half:] + rb1[0, d].astype(F32) + rb2[d].astype(F32)
        return first, last

    def third_send(d):
        first, last = third(d)
        s3[d, 0] = first.astype(BF16)
        s3[d, 1] = last.astype(BF16)
        copy_z(d).start()

    def turn(t):
        return jnp.where(t < 2, t + 2, 3 - t)

    def sum_step(t, carry):
        @pl.when(t < 4)
        def _():
            d = turn(t)
            both_far(d)
            one_far(d)
            near(d)

        @pl.when(t >= 1)
        def _():
            second(turn(t - 1))

        @pl.when(t >= 2)
        def _():
            third_send(turn(t - 2))

        return carry

    lax.fori_loop(0, 5, sum_step, 0)
    first, last = third(0)
    for d in (2, 3, 1):
        copy_z(d).wait_recv()
        first += r3[d, 0].astype(F32)
        last += r3[d, 1].astype(F32)
    basis_out[:, :half] = first
    basis_out[:, half:] = last
    gath[e, 0] = first.astype(BF16)
    gath[e, 1] = last.astype(BF16)

    def held(d, yr, xr):
        return chunk(z_of(d), yr, xr)

    def pass_on(c, part, sem, at, where):
        return remote(gath.at[c, part], gath.at[c, part], sem, at, where)

    copy_gz = lambda d: remote(gath.at[e], gath.at[e], gz_sem, (d,), to_z(d))
    copy_ga1 = lambda d: pass_on(held(d, 0, 0), 0, ga1_sem, (d,), to_y)
    copy_gb1 = lambda d: pass_on(held(d, 0, 0), 1, gb1_sem, (d,), to_x)
    copy_ga2 = lambda yr, d: pass_on(held(d, yr, 0), 0, ga2_sem, (yr, d), to_x)
    copy_gb2 = lambda xr, d: pass_on(held(d, 0, xr), 1, gb2_sem, (xr, d), to_y)

    def came_z(d):
        c = held(d, 0, 0)
        return remote(gath.at[c], gath.at[c], gz_sem, (d,), to_z(d))

    def came_a1(d):
        return pass_on(held(d, 1, 0), 0, ga1_sem, (d,), to_y)

    def came_b1(d):
        return pass_on(held(d, 0, 1), 1, gb1_sem, (d,), to_x)

    def came_a2(yr, d):
        return pass_on(held(d, yr, 1), 0, ga2_sem, (yr, d), to_x)

    def came_b2(xr, d):
        return pass_on(held(d, 1, xr), 1, gb2_sem, (xr, d), to_y)

    for d in (1, 2, 3):
        copy_gz(d).start()
    coef[...] = jnp.zeros_like(coef)

    def add_coef(c):
        block = jnp.concatenate([gath[c, 0], gath[c, 1]], axis=1)
        value = contract0(block, w_rows(c))
        width = value.shape[1] // 2
        coef[0] += value[:, :width]
        coef[1] += value[:, width:]

    def hand_out(d):
        copy_ga1(d).start()
        copy_gb1(d).start()
        copy_ga2(0, d).start()
        copy_gb2(0, d).start()

    def take_near(d):
        came_b2(0, d).wait_recv()
        add_coef(held(d, 1, 0))
        came_a2(0, d).wait_recv()
        add_coef(held(d, 0, 1))

    def gather_step(d, carry):
        @pl.when(d >= 1)
        def _():
            came_z(d).wait_recv()

        hand_out(d)
        add_coef(held(d, 0, 0))
        came_a1(d).wait_recv()
        copy_ga2(1, d).start()
        came_b1(d).wait_recv()
        copy_gb2(1, d).start()

        @pl.when(d >= 1)
        def _():
            take_near(d - 1)

        return carry

    lax.fori_loop(0, 4, gather_step, 0)
    take_near(3)

    def take_far(d, carry):
        came_a2(1, d).wait_recv()
        came_b2(1, d).wait_recv()
        add_coef(held(d, 1, 1))
        return carry

    lax.fori_loop(0, 4, take_far, 0)

    share = remote(coef.at[1 - s], c_recv, c_sem, (), to_core)
    share.start()

    def drain(d, carry):
        for k in (0, 1):
            copy_a1(k, d).wait_send()
            copy_b1(k, d).wait_send()
            copy_ga2(k, d).wait_send()
            copy_gb2(k, d).wait_send()
        copy_a2(d).wait_send()
        copy_b2(d).wait_send()
        copy_ga1(d).wait_send()
        copy_gb1(d).wait_send()
        return carry

    lax.fori_loop(0, 4, drain, 0)
    for d in (1, 2, 3):
        copy_z(d).wait_send()
        copy_gz(d).wait_send()
    for q in range(1, 8):
        copy_rows(0, q).wait_send()
        copy_rows(1, q).wait_send()
    for copy in (across, hand, copy_gs(0), copy_gs(1), cross, spread):
        copy.wait_send()
    share.wait()
    coef_out[...] = coef[s] + c_recv[...]


def panel_call(weight, probe, ids, tokens, row_mean):
    depth, width = weight.shape
    cols = probe.shape[1]
    cap = tokens.shape[0] // 8
    rows, half = depth // 16, cols // 2
    dma = pltpu.SemaphoreType.DMA
    vmem = pltpu.VMEM
    return pl.pallas_call(
        functools.partial(panel_kernel, row_mean),
        out_shape=(
            jax.ShapeDtypeStruct((rows, cols), F32),
            jax.ShapeDtypeStruct((cols, width // 2), F32),
        ),
        in_specs=[pl.BlockSpec(memory_space=pl.ANY)] * 3 + [pl.BlockSpec(memory_space=vmem)],
        out_specs=[pl.BlockSpec(memory_space=vmem)] * 2,
        scratch_shapes=[
            vmem(tokens.shape, BF16),
            vmem((depth, width), BF16),
            vmem((depth, cols), BF16),
            vmem((2, 8, cap, width), BF16),
            vmem((2, 8, cap, width), BF16),
            vmem((cols, width), F32),
            vmem((cols, width), F32),
            vmem((2, 2, half, width), BF16),
            vmem((2, 2, half, width), F32),
            vmem((2, half, width), F32),
            vmem((half, width), BF16),
            vmem((half, width), BF16),
            vmem((2, half, width), BF16),
            vmem((2, 4, rows, half), BF16),
            vmem((2, 4, rows, half), BF16),
            vmem((2, 4, rows, half), BF16),
            vmem((2, 4, rows, half), BF16),
            vmem((4, rows, half), F32),
            vmem((4, rows, half), F32),
            vmem((4, rows, cols), F32),
            vmem((4, rows, half), BF16),
            vmem((4, rows, half), BF16),
            vmem((4, rows, half), BF16),
            vmem((4, rows, half), BF16),
            vmem((4, 2, rows, half), BF16),
            vmem((4, 2, rows, half), BF16),
            vmem((16, 2, rows, half), BF16),
            vmem((2, cols, width // 2), F32),
            vmem((cols, width // 2), F32),
            dma((3,)),
            dma((2, 2, 8)),
            dma((2,)),
            dma((2,)),
            dma((2,)),
            dma((2, 2)),
            dma((2,)),
            dma((2,)),
            dma((2, 2, 4)),
            dma((2, 2, 4)),
            dma((2, 4)),
            dma((2, 4)),
            dma((2, 4)),
            dma((2, 4)),
            dma((2, 4)),
            dma((2, 4)),
            dma((2, 2, 4)),
            dma((2, 2, 4)),
            dma((2,)),
        ],
        compiler_params=pltpu.CompilerParams(
            collective_id=0, has_side_effects=True, vmem_limit_bytes=52 * 2**20
        ),
        cost_estimate=pl.CostEstimate(
            flops=8 * depth * width * cols, bytes_accessed=2 * depth * width, transcendentals=0
        ),
    )(weight, probe, tokens, ids)


def body(hidden_rows, routes, down_weight, probe):
    weight = down_weight[0]
    tok_count, top_count = routes.shape
    feature_width = hidden_rows.shape[2]
    experts = lax.axis_size("expert")
    capacity = 2 * tok_count * top_count // experts
    row_mean = tok_count * top_count * lax.axis_size("seq")
    if experts == 16 and lax.axis_size("seq") == 2:
        ids = routes.reshape(1, -1)
        tokens = hidden_rows.reshape(-1, feature_width)
        basis_rows, coefficients = panel_call(weight, probe, ids, tokens, row_mean)
        return (basis_rows, coefficients[None])
    partial_value = lax.dot_general(
        weight, probe, (((0,), (0,)), ((), ())), preferred_element_type=jnp.float32
    )
    probe_proj = lax.psum(partial_value, "seq").astype(jnp.bfloat16)
    expert_ids = routes.reshape(-1)
    onehot = (expert_ids[:, None] == jnp.arange(experts, dtype=jnp.int32)[None, :]).astype(
        jnp.int32
    )
    position = jnp.sum(onehot * (jnp.cumsum(onehot, axis=0) - 1), axis=1)
    destination = expert_ids * capacity + position
    outgoing = jnp.zeros((experts * capacity, feature_width), jnp.bfloat16)
    outgoing = outgoing.at[destination].set(hidden_rows.reshape(-1, feature_width))
    outgoing = outgoing.reshape(experts, capacity, feature_width)
    arrived = lax.all_to_all(outgoing, "expert", split_axis=0, concat_axis=0, tiled=True)
    arrived_rows = arrived.reshape(-1, feature_width)
    mixed = jnp.dot(arrived_rows, probe_proj, preferred_element_type=jnp.float32).astype(
        jnp.bfloat16
    )
    gram_part = lax.dot_general(
        arrived_rows, mixed, (((0,), (0,)), ((), ())), preferred_element_type=jnp.float32
    )
    gram_full = lax.psum(gram_part, "seq") / row_mean
    panel_image = jnp.dot(
        weight, gram_full.astype(jnp.bfloat16), preferred_element_type=jnp.float32
    )
    basis_rows = lax.psum_scatter(panel_image, "expert", scatter_dimension=0, tiled=True)
    coef_part = lax.dot_general(
        lax.all_gather(basis_rows.astype(jnp.bfloat16), "expert", axis=0, tiled=True),
        weight,
        (((0,), (0,)), ((), ())),
        preferred_element_type=jnp.float32,
    )
    coefficients = lax.psum_scatter(coef_part, "seq", scatter_dimension=1, tiled=True)
    return (basis_rows, coefficients[None])


def solution(mesh):
    in_specs = (
        P(("expert", "seq"), None, None),
        P(("expert", "seq"), None),
        P("expert", "seq", None),
        P("seq", None),
    )
    out_specs = (P(("seq", "expert"), None), P("expert", None, "seq"))
    return jax.shard_map(body, mesh=mesh, in_specs=in_specs, out_specs=out_specs, check_vma=False)
```

```python
import functools

import jax
import jax.numpy as jnp
from jax import lax
from jax.experimental import pallas as pl
from jax.experimental.pallas import tpu as pltpu
from jax.sharding import PartitionSpec as P

MESH = pl.DeviceIdType.MESH
F32 = jnp.float32
BF16 = jnp.bfloat16


def contract0(a, b):
    return lax.dot_general(a, b, (((0,), (0,)), ((), ())), preferred_element_type=F32)


def contract1(a, b):
    return lax.dot_general(a, b, (((1,), (1,)), ((), ())), preferred_element_type=F32)


def panel_kernel(
    row_mean, w_any, probe_any, tokens_any, routes, basis_out, coef_out,
    tokens, w, probe, sent, arr, p_part, p_recv, pt, gt, gr, sp, rp, g_bf, sa1, sb1, ra1, rb1, pa2, pb2, p3, sa2, sb2, ra2, rb2, s3, r3, gath, coef, c_recv,
    load_sem, rows_sem, p_sem, px_sem, po_sem, pf_sem, gs_sem, gx_sem, gf_sem, a1_sem, b1_sem, a2_sem, b2_sem, z_sem, gz_sem, ga1_sem, gb1_sem, ga2_sem, gb2_sem, c_sem,
):
    e, s = lax.axis_index("expert"), lax.axis_index("seq")
    x, y, z = e % 2, (e // 2) % 2, e // 4
    to_x = {"expert": e + 1 - 2 * x}
    to_y = {"expert": e + 2 - 4 * y}
    to_core = {"seq": 1 - s}

    def z_of(k):
        return (z // 2 + k // 2) % 2 * 2 + (z + k) % 2

    def to_z(k):
        return {"expert": z_of(k) * 4 + e % 4}

    rows, half = basis_out.shape[0], basis_out.shape[1] // 2

    def chunk(zz, yr, xr):
        return zz * 4 + ((y + yr) % 2) * 2 + (x + xr) % 2

    def w_rows(c):
        return w[pl.ds(pl.multiple_of(c * rows, rows), rows), :]

    def remote(src, dst, sem, at, where):
        return pltpu.make_async_remote_copy(
            src_ref=src, dst_ref=dst, send_sem=sem.at[(0, *at)], recv_sem=sem.at[(1, *at)],
            device_id=where, device_id_type=MESH,
        )

    top, cap = routes.shape
    own_half = z // 2
    partner = {"expert": (e + 8) % 16}

    def near_chip(q):
        return own_half * 8 + (z + q // 4) % 2 * 4 + (y + q // 2) % 2 * 2 + (x + q) % 2

    load_w = pltpu.make_async_copy(w_any, w, load_sem.at[0])
    load_probe = pltpu.make_async_copy(probe_any, probe, load_sem.at[1])
    load_tokens = pltpu.make_async_copy(tokens_any, tokens, load_sem.at[2])
    load_tokens.start()
    load_w.start()
    load_probe.start()

    barrier = pltpu.get_barrier_semaphore()
    for q in range(1, 8):
        pl.semaphore_signal(
            barrier, inc=1, device_id={"expert": near_chip(q)}, device_id_type=MESH
        )
    far = [{"expert": (2 - 2 * own_half + k) * 4 + e % 4} for k in (0, 1)]
    for where in (to_core, *far):
        pl.semaphore_signal(barrier, inc=1, device_id=where, device_id_type=MESH)

    amount = tokens.shape[0]
    lane = lax.broadcasted_iota(jnp.int32, (cap, amount), 1)
    token = lax.broadcasted_iota(jnp.int32, (cap, amount), 0)
    inside = lane - token * top
    widen = jnp.where((inside >= 0) & (inside < top), 1.0, 0.0).astype(BF16)
    wide = jnp.dot(routes[...].astype(F32).astype(BF16), widen, preferred_element_type=F32)
    turn_at = lax.rem(lax.broadcasted_iota(jnp.int32, (top, amount), 1), top)
    line_at = lax.broadcasted_iota(jnp.int32, (top, amount), 0)
    names = jnp.sum(jnp.where(turn_at == line_at, wide, 0.0), axis=0, keepdims=True).astype(jnp.int32)
    mark = (lax.broadcasted_iota(jnp.int32, (16, amount), 0) == names).astype(F32)
    before = (
        lax.broadcasted_iota(jnp.int32, (amount, amount), 0)
        < lax.broadcasted_iota(jnp.int32, (amount, amount), 1)
    ).astype(F32).astype(BF16)
    rank = jnp.dot(mark.astype(BF16), before, preferred_element_type=F32)
    place = jnp.sum(mark * rank, axis=0, keepdims=True).astype(jnp.int32) + names * cap

    def slot_chip(i):
        return near_chip(5 * i % 8)

    copy_rows = lambda k, i: remote(
        sent.at[k, i], arr.at[k, i], rows_sem, (k, i), {"expert": slot_chip(i)}
    )

    def block_for(i):
        chip = slot_chip(i)
        line = lax.broadcasted_iota(jnp.int32, (2 * cap, amount), 0)
        wanted = jnp.where(line < cap, chip * cap + line, ((chip + 8) % 16 - 1) * cap + line)
        pick = (wanted == place).astype(F32).astype(BF16)
        return jnp.dot(pick, tokens[...], preferred_element_type=F32).astype(BF16)

    load_tokens.wait()
    pl.semaphore_wait(barrier, 10)

    def send_rows(j, carry):
        i = j + 1
        block = block_for(i)
        sent[0, i] = block[:cap]
        copy_rows(0, i).start()
        sent[1, i] = block[cap:]
        copy_rows(1, i).start()
        return carry

    lax.fori_loop(0, 7, send_rows, 0)
    block = block_for(0)
    arr[0, 0] = block[:cap]
    arr[1, 0] = block[cap:]

    load_probe.wait()
    load_w.wait()
    p_part[...] = jnp.zeros_like(p_part)
    part = 512

    def project(i, carry):
        at = pl.ds(pl.multiple_of(i * part, part), part)
        p_part[...] += contract0(probe[at, :], w[at, :]).reshape(p_part.shape)
        return carry

    lax.fori_loop(0, w.shape[0] // part, project, 0)
    swap = remote(p_part.at[1 - s], p_recv, p_sem, (), to_core)
    swap.start()
    swap.wait_recv()
    pt[0, s] = (p_part[s] + p_recv[...]).astype(BF16)
    across = remote(pt.at[0, s], pt.at[1, s], px_sem, (), partner)
    across.start()
    own = remote(pt.at[0, s], pt.at[0, s], po_sem, (), to_core)
    own.start()
    remote(pt.at[0, 1 - s], pt.at[0, 1 - s], po_sem, (), to_core).wait_recv()

    def gram_of(k, first):
        rows_k = arr[k, first:first + 4].reshape(4 * cap, arr.shape[3])
        proj = pt[k].reshape(2 * pt.shape[2], pt.shape[3])
        mixed = contract1(rows_k, proj).astype(BF16)
        return contract0(mixed, rows_k).reshape(gt.shape[1:])

    for q in (1, 2, 3):
        copy_rows(0, q).wait_recv()
    gt[0] = gram_of(0, 0)
    across.wait_recv()
    hand = remote(pt.at[1, s], pt.at[1, s], pf_sem, (), to_core)
    hand.start()
    for q in (1, 2, 3):
        copy_rows(1, q).wait_recv()
    remote(pt.at[1, 1 - s], pt.at[1, 1 - s], pf_sem, (), to_core).wait_recv()
    gt[1] = gram_of(1, 0)
    for q in (4, 5, 6, 7):
        copy_rows(1, q).wait_recv()
    gt[1] += gram_of(1, 4)
    copy_gs = lambda k, g: remote(gt.at[k, g, 1 - s], gr.at[k, g], gs_sem, (k, g), to_core)
    cross = lambda g: remote(sp.at[g], rp.at[g], gx_sem, (g,), partner)
    spread = lambda g: remote(g_bf.at[g, s], g_bf.at[g, s], gf_sem, (g,), to_core)
    for g in (0, 1):
        copy_gs(1, g).start()
    for g in (0, 1):
        copy_gs(1, g).wait_recv()
        sp[g] = (gt[1, g, s] + gr[1, g]).astype(BF16)
        cross(g).start()
    for q in (4, 5, 6, 7):
        copy_rows(0, q).wait_recv()
    gt[0] += gram_of(0, 4)
    for g in (0, 1):
        copy_gs(0, g).start()

    def finish_gram(g):
        copy_gs(0, g).wait_recv()
        cross(g).wait_recv()
        total = gt[0, g, s] + gr[0, g] + rp[g].astype(F32)
        g_bf[g, s] = (total / row_mean).astype(BF16)
        spread(g).start()
        remote(g_bf.at[g, 1 - s], g_bf.at[g, 1 - s], gf_sem, (g,), to_core).wait_recv()

    finish_gram(0)

    part = rows // 2

    def panel(g, d, yr, xr):
        return contract1(w_rows(chunk(z_of(d), yr, xr)), g_bf[g].reshape(half, g_bf.shape[3]))

    copy_a1 = lambda g, yr, d: remote(sa1.at[g, yr, d], ra1.at[g, yr, d], a1_sem, (g, yr, d), to_x)
    copy_b1 = lambda g, xr, d: remote(sb1.at[g, xr, d], rb1.at[g, xr, d], b1_sem, (g, xr, d), to_y)
    copy_a2 = lambda g, d: remote(sa2.at[g, d], ra2.at[g, d], a2_sem, (g, d), to_y)
    copy_b2 = lambda g, d: remote(sb2.at[g, d], rb2.at[g, d], b2_sem, (g, d), to_x)
    copy_z = lambda g, d: remote(s3.at[g, d], r3.at[g, d], z_sem, (g, d), to_z(d))

    def first_stage(g, d):
        value = panel(g, d, 1, 1)
        sa1[g, 1, d] = value[:part].astype(BF16)
        copy_a1(g, 1, d).start()
        sb1[g, 1, d] = value[part:].astype(BF16)
        copy_b1(g, 1, d).start()
        value = panel(g, d, 0, 1)
        sa1[g, 0, d] = value[:part].astype(BF16)
        copy_a1(g, 0, d).start()
        pb2[g, d] = value[part:]
        value = panel(g, d, 1, 0)
        sb1[g, 0, d] = value[part:].astype(BF16)
        copy_b1(g, 0, d).start()
        pa2[g, d] = value[:part]
        p3[g, d] = panel(g, d, 0, 0)

    def second_stage(g, d):
        copy_a1(g, 1, d).wait_recv()
        sa2[g, d] = (pa2[g, d] + ra1[g, 1, d].astype(F32)).astype(BF16)
        copy_a2(g, d).start()
        copy_b1(g, 1, d).wait_recv()
        sb2[g, d] = (pb2[g, d] + rb1[g, 1, d].astype(F32)).astype(BF16)
        copy_b2(g, d).start()

    def third_stage(g, d):
        copy_a1(g, 0, d).wait_recv()
        copy_a2(g, d).wait_recv()
        p3[g, d, :part] += ra1[g, 0, d].astype(F32) + ra2[g, d].astype(F32)
        copy_b1(g, 0, d).wait_recv()
        copy_b2(g, d).wait_recv()
        p3[g, d, part:] += rb1[g, 0, d].astype(F32) + rb2[g, d].astype(F32)

        @pl.when(d != 0)
        def _():
            s3[g, d] = p3[g, d].astype(BF16).reshape(s3.shape[2:])
            copy_z(g, d).start()

    def item(t):
        i = t % 4
        return t // 4, jnp.where(i < 2, i + 2, 3 - i)

    def sum_step(t, carry):
        @pl.when(t == 4)
        def _():
            finish_gram(1)

        @pl.when(t < 8)
        def _():
            first_stage(*item(t))

        @pl.when((t >= 1) & (t < 9))
        def _():
            second_stage(*item(t - 1))

        @pl.when(t >= 2)
        def _():
            third_stage(*item(t - 2))

        return carry

    lax.fori_loop(0, 10, sum_step, 0)
    for g in (0, 1):
        total = p3[g, 0]
        for d in (2, 3, 1):
            copy_z(g, d).wait_recv()
            total += r3[g, d].astype(F32).reshape(rows, half)
        basis_out[:, g * half:(g + 1) * half] = total
        gath[e, :, :, g * half:(g + 1) * half] = total.astype(BF16).reshape(2, part, half)

    def held(d, yr, xr):
        return chunk(z_of(d), yr, xr)

    def pass_on(c, part, sem, at, where):
        return remote(gath.at[c, part], gath.at[c, part], sem, at, where)

    copy_gz = lambda d: remote(gath.at[e], gath.at[e], gz_sem, (d,), to_z(d))
    copy_ga1 = lambda d: pass_on(held(d, 0, 0), 0, ga1_sem, (d,), to_y)
    copy_gb1 = lambda d: pass_on(held(d, 0, 0), 1, gb1_sem, (d,), to_x)
    copy_ga2 = lambda yr, d: pass_on(held(d, yr, 0), 0, ga2_sem, (yr, d), to_x)
    copy_gb2 = lambda xr, d: pass_on(held(d, 0, xr), 1, gb2_sem, (xr, d), to_y)

    def came_z(d):
        c = held(d, 0, 0)
        return remote(gath.at[c], gath.at[c], gz_sem, (d,), to_z(d))

    def came_a1(d):
        return pass_on(held(d, 1, 0), 0, ga1_sem, (d,), to_y)

    def came_b1(d):
        return pass_on(held(d, 0, 1), 1, gb1_sem, (d,), to_x)

    def came_a2(yr, d):
        return pass_on(held(d, yr, 1), 0, ga2_sem, (yr, d), to_x)

    def came_b2(xr, d):
        return pass_on(held(d, 1, xr), 1, gb2_sem, (xr, d), to_y)

    for d in (1, 2, 3):
        copy_gz(d).start()
    coef[...] = jnp.zeros_like(coef)

    def add_coef(c):
        block = gath[c].reshape(rows, gath.shape[3])
        value = contract0(block, w_rows(c))
        width = value.shape[1] // 2
        coef[0] += value[:, :width]
        coef[1] += value[:, width:]

    def hand_out(d):
        copy_ga1(d).start()
        copy_gb1(d).start()
        copy_ga2(0, d).start()
        copy_gb2(0, d).start()

    def take_near(d):
        came_b2(0, d).wait_recv()
        add_coef(held(d, 1, 0))
        came_a2(0, d).wait_recv()
        add_coef(held(d, 0, 1))

    def gather_step(d, carry):
        @pl.when(d >= 1)
        def _():
            came_z(d).wait_recv()

        hand_out(d)
        add_coef(held(d, 0, 0))
        came_a1(d).wait_recv()
        copy_ga2(1, d).start()
        came_b1(d).wait_recv()
        copy_gb2(1, d).start()

        @pl.when(d >= 1)
        def _():
            take_near(d - 1)

        return carry

    lax.fori_loop(0, 4, gather_step, 0)
    take_near(3)

    def take_far(d, carry):
        came_a2(1, d).wait_recv()
        came_b2(1, d).wait_recv()
        add_coef(held(d, 1, 1))
        return carry

    lax.fori_loop(0, 4, take_far, 0)

    share = remote(coef.at[1 - s], c_recv, c_sem, (), to_core)
    share.start()

    def drain(d, carry):
        for k in (0, 1):
            for g in (0, 1):
                copy_a1(g, k, d).wait_send()
                copy_b1(g, k, d).wait_send()
            copy_a2(k, d).wait_send()
            copy_b2(k, d).wait_send()
            copy_ga2(k, d).wait_send()
            copy_gb2(k, d).wait_send()
        copy_ga1(d).wait_send()
        copy_gb1(d).wait_send()
        return carry

    lax.fori_loop(0, 4, drain, 0)
    for d in (1, 2, 3):
        copy_z(0, d).wait_send()
        copy_z(1, d).wait_send()
        copy_gz(d).wait_send()
    for q in range(1, 8):
        copy_rows(0, q).wait_send()
        copy_rows(1, q).wait_send()
    for copy in (swap, across, own, hand):
        copy.wait_send()
    for g in (0, 1):
        for copy in (copy_gs(0, g), copy_gs(1, g), cross(g), spread(g)):
            copy.wait_send()
    share.wait()
    coef_out[...] = coef[s] + c_recv[...]


def panel_call(weight, probe, routes, tokens, row_mean):
    depth, width = weight.shape
    cols = probe.shape[1]
    cap = routes.shape[1]
    rows, half = depth // 16, cols // 2
    part, quarter = rows // 2, half // 2
    dma = pltpu.SemaphoreType.DMA
    vmem = pltpu.VMEM
    return pl.pallas_call(
        functools.partial(panel_kernel, row_mean),
        out_shape=(
            jax.ShapeDtypeStruct((rows, cols), F32),
            jax.ShapeDtypeStruct((cols, width // 2), F32),
        ),
        in_specs=[pl.BlockSpec(memory_space=pl.ANY)] * 3 + [pl.BlockSpec(memory_space=vmem)],
        out_specs=[pl.BlockSpec(memory_space=vmem)] * 2,
        scratch_shapes=[
            vmem(tokens.shape, BF16),
            vmem((depth, width), BF16),
            vmem((depth, cols), BF16),
            vmem((2, 8, cap, width), BF16),
            vmem((2, 8, cap, width), BF16),
            vmem((2, half, width), F32),
            vmem((half, width), F32),
            vmem((2, 2, half, width), BF16),
            vmem((2, 2, 2, quarter, width), F32),
            vmem((2, 2, quarter, width), F32),
            vmem((2, quarter, width), BF16),
            vmem((2, quarter, width), BF16),
            vmem((2, 2, quarter, width), BF16),
            vmem((2, 2, 4, part, half), BF16),
            vmem((2, 2, 4, part, half), BF16),
            vmem((2, 2, 4, part, half), BF16),
            vmem((2, 2, 4, part, half), BF16),
            vmem((2, 4, part, half), F32),
            vmem((2, 4, part, half), F32),
            vmem((2, 4, rows, half), F32),
            vmem((2, 4, part, half), BF16),
            vmem((2, 4, part, half), BF16),
            vmem((2, 4, part, half), BF16),
            vmem((2, 4, part, half), BF16),
            vmem((2, 4, 2, part, half), BF16),
            vmem((2, 4, 2, part, half), BF16),
            vmem((16, 2, part, cols), BF16),
            vmem((2, cols, width // 2), F32),
            vmem((cols, width // 2), F32),
            dma((3,)),
            dma((2, 2, 8)),
            dma((2,)),
            dma((2,)),
            dma((2,)),
            dma((2,)),
            dma((2, 2, 2)),
            dma((2, 2)),
            dma((2, 2)),
            dma((2, 2, 2, 4)),
            dma((2, 2, 2, 4)),
            dma((2, 2, 4)),
            dma((2, 2, 4)),
            dma((2, 2, 4)),
            dma((2, 4)),
            dma((2, 4)),
            dma((2, 4)),
            dma((2, 2, 4)),
            dma((2, 2, 4)),
            dma((2,)),
        ],
        compiler_params=pltpu.CompilerParams(
            collective_id=0, has_side_effects=True, vmem_limit_bytes=127 * 2**19
        ),
        cost_estimate=pl.CostEstimate(
            flops=8 * depth * width * cols, bytes_accessed=2 * depth * width, transcendentals=0
        ),
    )(weight, probe, tokens, routes)


def body(hidden_rows, routes, down_weight, probe):
    weight = down_weight[0]
    tok_count, top_count = routes.shape
    feature_width = hidden_rows.shape[2]
    experts = lax.axis_size("expert")
    capacity = 2 * tok_count * top_count // experts
    row_mean = tok_count * top_count * lax.axis_size("seq")
    if experts == 16 and lax.axis_size("seq") == 2:
        tokens = hidden_rows.reshape(-1, feature_width)
        basis_rows, coefficients = panel_call(weight, probe, routes.T, tokens, row_mean)
        return (basis_rows, coefficients[None])
    partial_value = lax.dot_general(
        weight, probe, (((0,), (0,)), ((), ())), preferred_element_type=jnp.float32
    )
    probe_proj = lax.psum(partial_value, "seq").astype(jnp.bfloat16)
    expert_ids = routes.reshape(-1)
    onehot = (expert_ids[:, None] == jnp.arange(experts, dtype=jnp.int32)[None, :]).astype(
        jnp.int32
    )
    position = jnp.sum(onehot * (jnp.cumsum(onehot, axis=0) - 1), axis=1)
    destination = expert_ids * capacity + position
    outgoing = jnp.zeros((experts * capacity, feature_width), jnp.bfloat16)
    outgoing = outgoing.at[destination].set(hidden_rows.reshape(-1, feature_width))
    outgoing = outgoing.reshape(experts, capacity, feature_width)
    arrived = lax.all_to_all(outgoing, "expert", split_axis=0, concat_axis=0, tiled=True)
    arrived_rows = arrived.reshape(-1, feature_width)
    mixed = jnp.dot(arrived_rows, probe_proj, preferred_element_type=jnp.float32).astype(
        jnp.bfloat16
    )
    gram_part = lax.dot_general(
        arrived_rows, mixed, (((0,), (0,)), ((), ())), preferred_element_type=jnp.float32
    )
    gram_full = lax.psum(gram_part, "seq") / row_mean
    panel_image = jnp.dot(
        weight, gram_full.astype(jnp.bfloat16), preferred_element_type=jnp.float32
    )
    basis_rows = lax.psum_scatter(panel_image, "expert", scatter_dimension=0, tiled=True)
    coef_part = lax.dot_general(
        lax.all_gather(basis_rows.astype(jnp.bfloat16), "expert", axis=0, tiled=True),
        weight,
        (((0,), (0,)), ((), ())),
        preferred_element_type=jnp.float32,
    )
    coefficients = lax.psum_scatter(coef_part, "seq", scatter_dimension=1, tiled=True)
    return (basis_rows, coefficients[None])


def solution(mesh):
    in_specs = (
        P(("expert", "seq"), None, None),
        P(("expert", "seq"), None),
        P("expert", "seq", None),
        P("seq", None),
    )
    out_specs = (P(("seq", "expert"), None), P("expert", None, "seq"))
    return jax.shard_map(body, mesh=mesh, in_specs=in_specs, out_specs=out_specs, check_vma=False)
```

```python
import functools

import jax
import jax.numpy as jnp
from jax import lax
from jax.experimental import pallas as pl
from jax.experimental.pallas import tpu as pltpu
from jax.sharding import PartitionSpec as P

MESH = pl.DeviceIdType.MESH
F32 = jnp.float32
BF16 = jnp.bfloat16


def contract0(a, b):
    return lax.dot_general(a, b, (((0,), (0,)), ((), ())), preferred_element_type=F32)


def contract1(a, b):
    return lax.dot_general(a, b, (((1,), (1,)), ((), ())), preferred_element_type=F32)


def panel_kernel(
    row_mean, w_any, probe_any, tokens_any, routes, basis_out, coef_out,
    tokens, w, probe, sent, arr, p_part, p_recv, pt, gt, gr, sp, rp, g_bf, sa1, sb1, ra1, rb1, pa2, pb2, whole, p3, sa2, sb2, ra2, rb2, s3, r3, gath, coef, c_recv,
    load_sem, rows_sem, p_sem, px_sem, po_sem, pf_sem, gs_sem, gx_sem, gf_sem, a1_sem, b1_sem, a2_sem, b2_sem, z_sem, gz_sem, ga1_sem, gb1_sem, ga2_sem, gb2_sem, c_sem,
):
    e, s = lax.axis_index("expert"), lax.axis_index("seq")
    x, y, z = e % 2, (e // 2) % 2, e // 4
    to_x = {"expert": e + 1 - 2 * x}
    to_y = {"expert": e + 2 - 4 * y}
    to_core = {"seq": 1 - s}

    def z_of(k):
        return (z // 2 + k // 2) % 2 * 2 + (z + k) % 2

    def to_z(k):
        return {"expert": z_of(k) * 4 + e % 4}

    rows, half = basis_out.shape[0], basis_out.shape[1] // 2

    def chunk(zz, yr, xr):
        return zz * 4 + ((y + yr) % 2) * 2 + (x + xr) % 2

    def w_rows(c):
        return w[pl.ds(pl.multiple_of(c * rows, rows), rows), :]

    def remote(src, dst, sem, at, where):
        return pltpu.make_async_remote_copy(
            src_ref=src, dst_ref=dst, send_sem=sem.at[(0, *at)], recv_sem=sem.at[(1, *at)],
            device_id=where, device_id_type=MESH,
        )

    top, cap = routes.shape
    own_half = z // 2
    partner = {"expert": (e + 8) % 16}

    def near_chip(q):
        return own_half * 8 + (z + q // 4) % 2 * 4 + (y + q // 2) % 2 * 2 + (x + q) % 2

    load_w = pltpu.make_async_copy(w_any, w, load_sem.at[0])
    load_probe = pltpu.make_async_copy(probe_any, probe, load_sem.at[1])
    load_tokens = pltpu.make_async_copy(tokens_any, tokens, load_sem.at[2])
    load_tokens.start()
    load_w.start()
    load_probe.start()

    barrier = pltpu.get_barrier_semaphore()
    for q in range(1, 8):
        pl.semaphore_signal(
            barrier, inc=1, device_id={"expert": near_chip(q)}, device_id_type=MESH
        )
    far = [{"expert": (2 - 2 * own_half + k) * 4 + e % 4} for k in (0, 1)]
    for where in (to_core, *far):
        pl.semaphore_signal(barrier, inc=1, device_id=where, device_id_type=MESH)

    amount = tokens.shape[0]
    lane = lax.broadcasted_iota(jnp.int32, (cap, amount), 1)
    token = lax.broadcasted_iota(jnp.int32, (cap, amount), 0)
    inside = lane - token * top
    widen = jnp.where((inside >= 0) & (inside < top), 1.0, 0.0).astype(BF16)
    wide = jnp.dot(routes[...].astype(F32).astype(BF16), widen, preferred_element_type=F32)
    turn_at = lax.rem(lax.broadcasted_iota(jnp.int32, (top, amount), 1), top)
    line_at = lax.broadcasted_iota(jnp.int32, (top, amount), 0)
    names = jnp.sum(jnp.where(turn_at == line_at, wide, 0.0), axis=0, keepdims=True).astype(jnp.int32)
    mark = (lax.broadcasted_iota(jnp.int32, (16, amount), 0) == names).astype(F32)
    before = (
        lax.broadcasted_iota(jnp.int32, (amount, amount), 0)
        < lax.broadcasted_iota(jnp.int32, (amount, amount), 1)
    ).astype(F32).astype(BF16)
    rank = jnp.dot(mark.astype(BF16), before, preferred_element_type=F32)
    place = jnp.sum(mark * rank, axis=0, keepdims=True).astype(jnp.int32) + names * cap

    def slot_chip(i):
        return near_chip(5 * i % 8)

    copy_rows = lambda k, i: remote(
        sent.at[k, i], arr.at[k, i], rows_sem, (k, i), {"expert": slot_chip(i)}
    )

    def blocks_for(slots):
        line = lax.broadcasted_iota(jnp.int32, (2 * cap, amount), 0)
        picks = []
        for i in slots:
            chip = slot_chip(i)
            wanted = jnp.where(line < cap, chip * cap + line, ((chip + 8) % 16 - 1) * cap + line)
            picks.append((wanted == place).astype(F32).astype(BF16))
        pick = jnp.concatenate(picks, axis=0)
        found = jnp.dot(pick, tokens[...], preferred_element_type=F32).astype(BF16)
        return found.reshape(len(slots), 2, cap, found.shape[1])

    load_tokens.wait()
    pl.semaphore_wait(barrier, 10)

    def send_rows(i, block):
        for k in (0, 1):
            sent[k, i] = block[k]
            copy_rows(k, i).start()

    def send_pair(j, carry):
        i = 2 * j + 1
        blocks = blocks_for((i, i + 1))
        send_rows(i, blocks[0])
        send_rows(i + 1, blocks[1])
        return carry

    lax.fori_loop(0, 3, send_pair, 0)
    blocks = blocks_for((7, 0))
    send_rows(7, blocks[0])
    arr[0, 0] = blocks[1, 0]
    arr[1, 0] = blocks[1, 1]

    load_probe.wait()
    load_w.wait()
    p_part[...] = jnp.zeros_like(p_part)
    part = 512

    def project(i, carry):
        at = pl.ds(pl.multiple_of(i * part, part), part)
        p_part[...] += contract0(probe[at, :], w[at, :]).reshape(p_part.shape)
        return carry

    lax.fori_loop(0, w.shape[0] // part, project, 0)
    swap = remote(p_part.at[1 - s], p_recv, p_sem, (), to_core)
    swap.start()
    swap.wait_recv()
    pt[0, s] = (p_part[s] + p_recv[...]).astype(BF16)
    across = remote(pt.at[0, s], pt.at[1, s], px_sem, (), partner)
    across.start()
    own = remote(pt.at[0, s], pt.at[0, s], po_sem, (), to_core)
    own.start()
    remote(pt.at[0, 1 - s], pt.at[0, 1 - s], po_sem, (), to_core).wait_recv()

    def gram_of(k, first):
        rows_k = arr[k, first:first + 4].reshape(4 * cap, arr.shape[3])
        proj = pt[k].reshape(2 * pt.shape[2], pt.shape[3])
        mixed = contract1(rows_k, proj).astype(BF16)
        return contract0(mixed, rows_k).reshape(gt.shape[1:])

    for q in (1, 2, 3):
        copy_rows(0, q).wait_recv()
    gt[0] = gram_of(0, 0)
    across.wait_recv()
    hand = remote(pt.at[1, s], pt.at[1, s], pf_sem, (), to_core)
    hand.start()
    for q in (1, 2, 3):
        copy_rows(1, q).wait_recv()
    remote(pt.at[1, 1 - s], pt.at[1, 1 - s], pf_sem, (), to_core).wait_recv()
    gt[1] = gram_of(1, 0)
    for q in (4, 5, 6, 7):
        copy_rows(1, q).wait_recv()
    gt[1] += gram_of(1, 4)
    copy_gs = lambda k, g: remote(gt.at[k, g, 1 - s], gr.at[k, g], gs_sem, (k, g), to_core)
    cross = lambda g: remote(sp.at[g], rp.at[g], gx_sem, (g,), partner)
    spread = lambda g: remote(g_bf.at[g, s], g_bf.at[g, s], gf_sem, (g,), to_core)
    for g in (0, 1):
        copy_gs(1, g).start()
    for g in (0, 1):
        copy_gs(1, g).wait_recv()
        sp[g] = (gt[1, g, s] + gr[1, g]).astype(BF16)
        cross(g).start()
    for q in (4, 5, 6, 7):
        copy_rows(0, q).wait_recv()
    gt[0] += gram_of(0, 4)
    for g in (0, 1):
        copy_gs(0, g).start()

    def finish_gram(g):
        copy_gs(0, g).wait_recv()
        cross(g).wait_recv()
        total = gt[0, g, s] + gr[0, g] + rp[g].astype(F32)
        g_bf[g, s] = (total / row_mean).astype(BF16)
        spread(g).start()
        remote(g_bf.at[g, 1 - s], g_bf.at[g, 1 - s], gf_sem, (g,), to_core).wait_recv()

    finish_gram(0)

    part = rows // 2

    copy_a1 = lambda g, yr, d: remote(sa1.at[g, yr, d], ra1.at[g, yr, d], a1_sem, (g, yr, d), to_x)
    copy_b1 = lambda g, xr, d: remote(sb1.at[g, xr, d], rb1.at[g, xr, d], b1_sem, (g, xr, d), to_y)
    copy_a2 = lambda g, d: remote(sa2.at[g, d], ra2.at[g, d], a2_sem, (g, d), to_y)
    copy_b2 = lambda g, d: remote(sb2.at[g, d], rb2.at[g, d], b2_sem, (g, d), to_x)
    copy_z = lambda g, d: remote(s3.at[g, d], r3.at[g, d], z_sem, (g, d), to_z(d))

    def first_stage(g, d):
        at = pl.ds(pl.multiple_of(z_of(d) * 4 * rows, rows), 4 * rows)
        value = contract1(w[at, :], g_bf[g].reshape(half, g_bf.shape[3]))
        whole[...] = value.reshape(whole.shape)
        place_of = lambda yr, xr: (y + yr) % 2 * 2 + (x + xr) % 2
        c = place_of(1, 1)
        sa1[g, 1, d] = whole[c, 0].astype(BF16)
        copy_a1(g, 1, d).start()
        sb1[g, 1, d] = whole[c, 1].astype(BF16)
        copy_b1(g, 1, d).start()
        c = place_of(0, 1)
        sa1[g, 0, d] = whole[c, 0].astype(BF16)
        copy_a1(g, 0, d).start()
        pb2[g, d] = whole[c, 1]
        c = place_of(1, 0)
        sb1[g, 0, d] = whole[c, 1].astype(BF16)
        copy_b1(g, 0, d).start()
        pa2[g, d] = whole[c, 0]
        p3[g, d] = whole[place_of(0, 0)].reshape(rows, half)

    def second_stage(g, d):
        copy_a1(g, 1, d).wait_recv()
        sa2[g, d] = (pa2[g, d] + ra1[g, 1, d].astype(F32)).astype(BF16)
        copy_a2(g, d).start()
        copy_b1(g, 1, d).wait_recv()
        sb2[g, d] = (pb2[g, d] + rb1[g, 1, d].astype(F32)).astype(BF16)
        copy_b2(g, d).start()

    def third_stage(g, d):
        copy_a1(g, 0, d).wait_recv()
        copy_a2(g, d).wait_recv()
        p3[g, d, :part] += ra1[g, 0, d].astype(F32) + ra2[g, d].astype(F32)
        copy_b1(g, 0, d).wait_recv()
        copy_b2(g, d).wait_recv()
        p3[g, d, part:] += rb1[g, 0, d].astype(F32) + rb2[g, d].astype(F32)

        @pl.when(d != 0)
        def _():
            s3[g, d] = p3[g, d].astype(BF16).reshape(s3.shape[2:])
            copy_z(g, d).start()

    def item(t):
        i = t % 4
        return t // 4, jnp.where(i < 2, i + 2, 3 - i)

    def sum_step(t, carry):
        @pl.when(t == 4)
        def _():
            finish_gram(1)

        @pl.when(t < 8)
        def _():
            first_stage(*item(t))

        @pl.when((t >= 1) & (t < 9))
        def _():
            second_stage(*item(t - 1))

        @pl.when(t >= 2)
        def _():
            third_stage(*item(t - 2))

        return carry

    lax.fori_loop(0, 10, sum_step, 0)
    for g in (0, 1):
        total = p3[g, 0]
        for d in (2, 3, 1):
            copy_z(g, d).wait_recv()
            total += r3[g, d].astype(F32).reshape(rows, half)
        basis_out[:, g * half:(g + 1) * half] = total
        gath[e, :, :, g * half:(g + 1) * half] = total.astype(BF16).reshape(2, part, half)

    def held(d, yr, xr):
        return chunk(z_of(d), yr, xr)

    def pass_on(c, part, sem, at, where):
        return remote(gath.at[c, part], gath.at[c, part], sem, at, where)

    copy_gz = lambda d: remote(gath.at[e], gath.at[e], gz_sem, (d,), to_z(d))
    copy_ga1 = lambda d: pass_on(held(d, 0, 0), 0, ga1_sem, (d,), to_y)
    copy_gb1 = lambda d: pass_on(held(d, 0, 0), 1, gb1_sem, (d,), to_x)
    copy_ga2 = lambda yr, d: pass_on(held(d, yr, 0), 0, ga2_sem, (yr, d), to_x)
    copy_gb2 = lambda xr, d: pass_on(held(d, 0, xr), 1, gb2_sem, (xr, d), to_y)

    def came_z(d):
        c = held(d, 0, 0)
        return remote(gath.at[c], gath.at[c], gz_sem, (d,), to_z(d))

    def came_a1(d):
        return pass_on(held(d, 1, 0), 0, ga1_sem, (d,), to_y)

    def came_b1(d):
        return pass_on(held(d, 0, 1), 1, gb1_sem, (d,), to_x)

    def came_a2(yr, d):
        return pass_on(held(d, yr, 1), 0, ga2_sem, (yr, d), to_x)

    def came_b2(xr, d):
        return pass_on(held(d, 1, xr), 1, gb2_sem, (xr, d), to_y)

    for d in (1, 2, 3):
        copy_gz(d).start()
    coef[...] = jnp.zeros_like(coef)

    def add_coef(c):
        block = gath[c].reshape(rows, gath.shape[3])
        value = contract0(block, w_rows(c))
        width = value.shape[1] // 2
        coef[0] += value[:, :width]
        coef[1] += value[:, width:]

    def hand_out(d):
        copy_ga1(d).start()
        copy_gb1(d).start()
        copy_ga2(0, d).start()
        copy_gb2(0, d).start()

    def take_near(d):
        came_b2(0, d).wait_recv()
        came_a2(0, d).wait_recv()

    def take_far(d):
        came_a2(1, d).wait_recv()
        came_b2(1, d).wait_recv()

    def add_whole(d):
        take_near(d)
        take_far(d)
        first = z_of(d) * 4
        block = gath[pl.ds(first, 4)].reshape(4 * rows, gath.shape[3])
        value = contract0(block, w[pl.ds(pl.multiple_of(first * rows, rows), 4 * rows), :])
        width = value.shape[1] // 2
        coef[0] += value[:, :width]
        coef[1] += value[:, width:]

    def gather_step(d, carry):
        @pl.when(d >= 1)
        def _():
            came_z(d).wait_recv()

        hand_out(d)

        @pl.when(d >= 2)
        def _():
            add_whole(d - 2)

        came_a1(d).wait_recv()
        copy_ga2(1, d).start()
        came_b1(d).wait_recv()
        copy_gb2(1, d).start()
        return carry

    lax.fori_loop(0, 4, gather_step, 0)
    add_coef(held(3, 0, 0))
    add_whole(2)
    take_near(3)
    add_coef(held(3, 1, 0))
    add_coef(held(3, 0, 1))
    take_far(3)
    add_coef(held(3, 1, 1))

    share = remote(coef.at[1 - s], c_recv, c_sem, (), to_core)
    share.start()

    def drain(d, carry):
        for k in (0, 1):
            for g in (0, 1):
                copy_a1(g, k, d).wait_send()
                copy_b1(g, k, d).wait_send()
            copy_a2(k, d).wait_send()
            copy_b2(k, d).wait_send()
            copy_ga2(k, d).wait_send()
            copy_gb2(k, d).wait_send()
        copy_ga1(d).wait_send()
        copy_gb1(d).wait_send()
        return carry

    lax.fori_loop(0, 4, drain, 0)
    for d in (1, 2, 3):
        copy_z(0, d).wait_send()
        copy_z(1, d).wait_send()
        copy_gz(d).wait_send()
    for q in range(1, 8):
        copy_rows(0, q).wait_send()
        copy_rows(1, q).wait_send()
    for copy in (swap, across, own, hand):
        copy.wait_send()
    for g in (0, 1):
        for copy in (copy_gs(0, g), copy_gs(1, g), cross(g), spread(g)):
            copy.wait_send()
    share.wait()
    coef_out[...] = coef[s] + c_recv[...]


def panel_call(weight, probe, routes, tokens, row_mean):
    depth, width = weight.shape
    cols = probe.shape[1]
    cap = routes.shape[1]
    rows, half = depth // 16, cols // 2
    part, quarter = rows // 2, half // 2
    dma = pltpu.SemaphoreType.DMA
    vmem = pltpu.VMEM
    return pl.pallas_call(
        functools.partial(panel_kernel, row_mean),
        out_shape=(
            jax.ShapeDtypeStruct((rows, cols), F32),
            jax.ShapeDtypeStruct((cols, width // 2), F32),
        ),
        in_specs=[pl.BlockSpec(memory_space=pltpu.HBM)] * 3 + [pl.BlockSpec(memory_space=vmem)],
        out_specs=[pl.BlockSpec(memory_space=vmem)] * 2,
        scratch_shapes=[
            vmem(tokens.shape, BF16),
            vmem((depth, width), BF16),
            vmem((depth, cols), BF16),
            vmem((2, 8, cap, width), BF16),
            vmem((2, 8, cap, width), BF16),
            vmem((2, half, width), F32),
            vmem((half, width), F32),
            vmem((2, 2, half, width), BF16),
            vmem((2, 2, 2, quarter, width), F32),
            vmem((2, 2, quarter, width), F32),
            vmem((2, quarter, width), BF16),
            vmem((2, quarter, width), BF16),
            vmem((2, 2, quarter, width), BF16),
            vmem((2, 2, 4, part, half), BF16),
            vmem((2, 2, 4, part, half), BF16),
            vmem((2, 2, 4, part, half), BF16),
            vmem((2, 2, 4, part, half), BF16),
            vmem((2, 4, part, half), F32),
            vmem((2, 4, part, half), F32),
            vmem((4, 2, part, half), F32),
            vmem((2, 4, rows, half), F32),
            vmem((2, 4, part, half), BF16),
            vmem((2, 4, part, half), BF16),
            vmem((2, 4, part, half), BF16),
            vmem((2, 4, part, half), BF16),
            vmem((2, 4, 2, part, half), BF16),
            vmem((2, 4, 2, part, half), BF16),
            vmem((16, 2, part, cols), BF16),
            vmem((2, cols, width // 2), F32),
            vmem((cols, width // 2), F32),
            dma((3,)),
            dma((2, 2, 8)),
            dma((2,)),
            dma((2,)),
            dma((2,)),
            dma((2,)),
            dma((2, 2, 2)),
            dma((2, 2)),
            dma((2, 2)),
            dma((2, 2, 2, 4)),
            dma((2, 2, 2, 4)),
            dma((2, 2, 4)),
            dma((2, 2, 4)),
            dma((2, 2, 4)),
            dma((2, 4)),
            dma((2, 4)),
            dma((2, 4)),
            dma((2, 2, 4)),
            dma((2, 2, 4)),
            dma((2,)),
        ],
        compiler_params=pltpu.CompilerParams(
            collective_id=0, has_side_effects=True, vmem_limit_bytes=52 * 2**20
        ),
        cost_estimate=pl.CostEstimate(
            flops=8 * depth * width * cols, bytes_accessed=2 * depth * width, transcendentals=0
        ),
    )(weight, probe, tokens, routes)


def body(hidden_rows, routes, down_weight, probe):
    weight = down_weight[0]
    tok_count, top_count = routes.shape
    feature_width = hidden_rows.shape[2]
    experts = lax.axis_size("expert")
    capacity = 2 * tok_count * top_count // experts
    row_mean = tok_count * top_count * lax.axis_size("seq")
    if experts == 16 and lax.axis_size("seq") == 2:
        tokens = hidden_rows.reshape(-1, feature_width)
        basis_rows, coefficients = panel_call(weight, probe, routes.T, tokens, row_mean)
        return (basis_rows, coefficients[None])
    partial_value = lax.dot_general(
        weight, probe, (((0,), (0,)), ((), ())), preferred_element_type=jnp.float32
    )
    probe_proj = lax.psum(partial_value, "seq").astype(jnp.bfloat16)
    expert_ids = routes.reshape(-1)
    onehot = (expert_ids[:, None] == jnp.arange(experts, dtype=jnp.int32)[None, :]).astype(
        jnp.int32
    )
    position = jnp.sum(onehot * (jnp.cumsum(onehot, axis=0) - 1), axis=1)
    destination = expert_ids * capacity + position
    outgoing = jnp.zeros((experts * capacity, feature_width), jnp.bfloat16)
    outgoing = outgoing.at[destination].set(hidden_rows.reshape(-1, feature_width))
    outgoing = outgoing.reshape(experts, capacity, feature_width)
    arrived = lax.all_to_all(outgoing, "expert", split_axis=0, concat_axis=0, tiled=True)
    arrived_rows = arrived.reshape(-1, feature_width)
    mixed = jnp.dot(arrived_rows, probe_proj, preferred_element_type=jnp.float32).astype(
        jnp.bfloat16
    )
    gram_part = lax.dot_general(
        arrived_rows, mixed, (((0,), (0,)), ((), ())), preferred_element_type=jnp.float32
    )
    gram_full = lax.psum(gram_part, "seq") / row_mean
    panel_image = jnp.dot(
        weight, gram_full.astype(jnp.bfloat16), preferred_element_type=jnp.float32
    )
    basis_rows = lax.psum_scatter(panel_image, "expert", scatter_dimension=0, tiled=True)
    coef_part = lax.dot_general(
        lax.all_gather(basis_rows.astype(jnp.bfloat16), "expert", axis=0, tiled=True),
        weight,
        (((0,), (0,)), ((), ())),
        preferred_element_type=jnp.float32,
    )
    coefficients = lax.psum_scatter(coef_part, "seq", scatter_dimension=1, tiled=True)
    return (basis_rows, coefficients[None])


def solution(mesh):
    in_specs = (
        P(("expert", "seq"), None, None),
        P(("expert", "seq"), None),
        P("expert", "seq", None),
        P("seq", None),
    )
    out_specs = (P(("seq", "expert"), None), P("expert", None, "seq"))
    return jax.shard_map(body, mesh=mesh, in_specs=in_specs, out_specs=out_specs, check_vma=False)
```

```python
import functools

import jax
import jax.numpy as jnp
from jax import lax
from jax.experimental import pallas as pl
from jax.experimental.pallas import tpu as pltpu
from jax.sharding import PartitionSpec as P

MESH = pl.DeviceIdType.MESH
F32 = jnp.float32
BF16 = jnp.bfloat16


def contract0(a, b):
    return lax.dot_general(a, b, (((0,), (0,)), ((), ())), preferred_element_type=F32)


def contract1(a, b):
    return lax.dot_general(a, b, (((1,), (1,)), ((), ())), preferred_element_type=F32)


def panel_kernel(
    row_mean, w_any, probe_any, tokens_any, routes, basis_out, coef_out,
    tokens, w, probe, sent, arr, p_part, p_recv, pt, gt, gr, sp, rp, g_bf, sa1, sb1, ra1, rb1, pa2, pb2, whole, p3, sa2, sb2, ra2, rb2, s3, r3, gath, coef, c_recv,
    load_sem, rows_sem, p_sem, px_sem, po_sem, pf_sem, gs_sem, gx_sem, gf_sem, a1_sem, b1_sem, a2_sem, b2_sem, z_sem, gz_sem, ga1_sem, gb1_sem, ga2_sem, gb2_sem, c_sem,
):
    e, s = lax.axis_index("expert"), lax.axis_index("seq")
    x, y, z = e % 2, (e // 2) % 2, e // 4
    to_x = {"expert": e + 1 - 2 * x}
    to_y = {"expert": e + 2 - 4 * y}
    to_core = {"seq": 1 - s}

    def z_of(k):
        return (z // 2 + k // 2) % 2 * 2 + (z + k) % 2

    def to_z(k):
        return {"expert": z_of(k) * 4 + e % 4}

    rows, half = basis_out.shape[0], basis_out.shape[1] // 2

    def chunk(zz, yr, xr):
        return zz * 4 + ((y + yr) % 2) * 2 + (x + xr) % 2

    def w_rows(c):
        return w[pl.ds(pl.multiple_of(c * rows, rows), rows), :]

    def remote(src, dst, sem, at, where):
        return pltpu.make_async_remote_copy(
            src_ref=src, dst_ref=dst, send_sem=sem.at[(0, *at)], recv_sem=sem.at[(1, *at)],
            device_id=where, device_id_type=MESH,
        )

    top, cap = routes.shape
    own_half = z // 2
    partner = {"expert": (e + 8) % 16}

    def near_chip(q):
        return own_half * 8 + (z + q // 4) % 2 * 4 + (y + q // 2) % 2 * 2 + (x + q) % 2

    load_w = pltpu.make_async_copy(w_any, w, load_sem.at[0])
    load_probe = pltpu.make_async_copy(probe_any, probe, load_sem.at[1])
    load_tokens = pltpu.make_async_copy(tokens_any, tokens, load_sem.at[2])
    load_tokens.start()
    load_w.start()
    load_probe.start()

    barrier = pltpu.get_barrier_semaphore()
    for q in range(1, 8):
        pl.semaphore_signal(
            barrier, inc=1, device_id={"expert": near_chip(q)}, device_id_type=MESH
        )
    far = [{"expert": (2 - 2 * own_half + k) * 4 + e % 4} for k in (0, 1)]
    for where in (to_core, *far):
        pl.semaphore_signal(barrier, inc=1, device_id=where, device_id_type=MESH)

    amount = tokens.shape[0]
    lane = lax.broadcasted_iota(jnp.int32, (cap, amount), 1)
    token = lax.broadcasted_iota(jnp.int32, (cap, amount), 0)
    inside = lane - token * top
    widen = jnp.where((inside >= 0) & (inside < top), 1.0, 0.0).astype(BF16)
    wide = jnp.dot(routes[...].astype(F32).astype(BF16), widen, preferred_element_type=F32)
    turn_at = lax.rem(lax.broadcasted_iota(jnp.int32, (top, amount), 1), top)
    line_at = lax.broadcasted_iota(jnp.int32, (top, amount), 0)
    names = jnp.sum(jnp.where(turn_at == line_at, wide, 0.0), axis=0, keepdims=True).astype(jnp.int32)
    mark = (lax.broadcasted_iota(jnp.int32, (16, amount), 0) == names).astype(F32)
    before = (
        lax.broadcasted_iota(jnp.int32, (amount, amount), 0)
        < lax.broadcasted_iota(jnp.int32, (amount, amount), 1)
    ).astype(F32).astype(BF16)
    rank = jnp.dot(mark.astype(BF16), before, preferred_element_type=F32)
    place = jnp.sum(mark * rank, axis=0, keepdims=True).astype(jnp.int32) + names * cap

    def slot_chip(i):
        return near_chip(5 * i % 8)

    copy_rows = lambda k, i: remote(
        sent.at[k, i], arr.at[k, i], rows_sem, (k, i), {"expert": slot_chip(i)}
    )

    def blocks_for(slots):
        line = lax.broadcasted_iota(jnp.int32, (2 * cap, amount), 0)
        picks = []
        for i in slots:
            chip = slot_chip(i)
            wanted = jnp.where(line < cap, chip * cap + line, ((chip + 8) % 16 - 1) * cap + line)
            picks.append((wanted == place).astype(F32).astype(BF16))
        pick = jnp.concatenate(picks, axis=0)
        found = jnp.dot(pick, tokens[...], preferred_element_type=F32).astype(BF16)
        return found.reshape(len(slots), 2, cap, found.shape[1])

    load_tokens.wait()
    pl.semaphore_wait(barrier, 10)

    def send_rows(i, block):
        for k in (0, 1):
            sent[k, i] = block[k]
            copy_rows(k, i).start()

    def send_pair(j, carry):
        i = 2 * j + 1
        blocks = blocks_for((i, i + 1))
        send_rows(i, blocks[0])
        send_rows(i + 1, blocks[1])
        return carry

    lax.fori_loop(0, 3, send_pair, 0)
    blocks = blocks_for((7, 0))
    send_rows(7, blocks[0])
    arr[0, 0] = blocks[1, 0]
    arr[1, 0] = blocks[1, 1]

    load_probe.wait()
    load_w.wait()
    p_part[...] = jnp.zeros_like(p_part)
    part = 512

    def project(i, carry):
        at = pl.ds(pl.multiple_of(i * part, part), part)
        p_part[...] += contract0(probe[at, :], w[at, :]).reshape(p_part.shape)
        return carry

    lax.fori_loop(0, w.shape[0] // part, project, 0)
    swap = remote(p_part.at[1 - s], p_recv, p_sem, (), to_core)
    swap.start()
    swap.wait_recv()
    pt[0, s] = (p_part[s] + p_recv[...]).astype(BF16)
    across = remote(pt.at[0, s], pt.at[1, s], px_sem, (), partner)
    across.start()
    own = remote(pt.at[0, s], pt.at[0, s], po_sem, (), to_core)
    own.start()
    remote(pt.at[0, 1 - s], pt.at[0, 1 - s], po_sem, (), to_core).wait_recv()

    def gram_of(k, first):
        rows_k = arr[k, first:first + 4].reshape(4 * cap, arr.shape[3])
        proj = pt[k].reshape(2 * pt.shape[2], pt.shape[3])
        mixed = contract1(rows_k, proj).astype(BF16)
        return contract0(mixed, rows_k).reshape(gt.shape[1:])

    for q in (1, 2, 3):
        copy_rows(0, q).wait_recv()
    gt[0] = gram_of(0, 0)
    across.wait_recv()
    hand = remote(pt.at[1, s], pt.at[1, s], pf_sem, (), to_core)
    hand.start()
    for q in (1, 2, 3):
        copy_rows(1, q).wait_recv()
    remote(pt.at[1, 1 - s], pt.at[1, 1 - s], pf_sem, (), to_core).wait_recv()
    gt[1] = gram_of(1, 0)
    for q in (4, 5, 6, 7):
        copy_rows(1, q).wait_recv()
    gt[1] += gram_of(1, 4)
    copy_gs = lambda k, g: remote(gt.at[k, g, 1 - s], gr.at[k, g], gs_sem, (k, g), to_core)
    cross = lambda g: remote(sp.at[g], rp.at[g], gx_sem, (g,), partner)
    spread = lambda g: remote(g_bf.at[g, s], g_bf.at[g, s], gf_sem, (g,), to_core)
    for g in (0, 1):
        copy_gs(1, g).start()
    copy_gs(1, 0).wait_recv()
    sp[0] = (gt[1, 0, s] + gr[1, 0]).astype(BF16)
    cross(0).start()
    for q in (4, 5, 6, 7):
        copy_rows(0, q).wait_recv()
    gt[0] += gram_of(0, 4)
    for g in (0, 1):
        copy_gs(0, g).start()

    def finish_gram(g):
        copy_gs(0, g).wait_recv()
        cross(g).wait_recv()
        total = gt[0, g, s] + gr[0, g] + rp[g].astype(F32)
        g_bf[g, s] = (total / row_mean).astype(BF16)
        spread(g).start()
        remote(g_bf.at[g, 1 - s], g_bf.at[g, 1 - s], gf_sem, (g,), to_core).wait_recv()

    copy_gs(1, 1).wait_recv()
    sp[1] = (gt[1, 1, s] + gr[1, 1]).astype(BF16)
    cross(0).wait_send()
    cross(1).start()
    finish_gram(0)

    part = rows // 2

    copy_a1 = lambda g, yr, d: remote(sa1.at[g, yr, d], ra1.at[g, yr, d], a1_sem, (g, yr, d), to_x)
    copy_b1 = lambda g, xr, d: remote(sb1.at[g, xr, d], rb1.at[g, xr, d], b1_sem, (g, xr, d), to_y)
    copy_a2 = lambda g, d: remote(sa2.at[g, d], ra2.at[g, d], a2_sem, (g, d), to_y)
    copy_b2 = lambda g, d: remote(sb2.at[g, d], rb2.at[g, d], b2_sem, (g, d), to_x)
    copy_z = lambda g, d: remote(s3.at[g, d], r3.at[g, d], z_sem, (g, d), to_z(d))

    def first_stage(g, d):
        at = pl.ds(pl.multiple_of(z_of(d) * 4 * rows, rows), 4 * rows)
        value = contract1(w[at, :], g_bf[g].reshape(half, g_bf.shape[3]))
        whole[...] = value.reshape(whole.shape)
        place_of = lambda yr, xr: (y + yr) % 2 * 2 + (x + xr) % 2
        c = place_of(1, 1)
        sa1[g, 1, d] = whole[c, 0].astype(BF16)
        copy_a1(g, 1, d).start()
        sb1[g, 1, d] = whole[c, 1].astype(BF16)
        copy_b1(g, 1, d).start()
        c = place_of(0, 1)
        sa1[g, 0, d] = whole[c, 0].astype(BF16)
        copy_a1(g, 0, d).start()
        pb2[g, d] = whole[c, 1]
        c = place_of(1, 0)
        sb1[g, 0, d] = whole[c, 1].astype(BF16)
        copy_b1(g, 0, d).start()
        pa2[g, d] = whole[c, 0]
        p3[g, d] = whole[place_of(0, 0)].reshape(rows, half)

    def second_stage(g, d):
        copy_a1(g, 1, d).wait_recv()
        sa2[g, d] = (pa2[g, d] + ra1[g, 1, d].astype(F32)).astype(BF16)
        copy_a2(g, d).start()
        copy_b1(g, 1, d).wait_recv()
        sb2[g, d] = (pb2[g, d] + rb1[g, 1, d].astype(F32)).astype(BF16)
        copy_b2(g, d).start()

    def third_stage(g, d):
        copy_a1(g, 0, d).wait_recv()
        copy_a2(g, d).wait_recv()
        p3[g, d, :part] += ra1[g, 0, d].astype(F32) + ra2[g, d].astype(F32)
        copy_b1(g, 0, d).wait_recv()
        copy_b2(g, d).wait_recv()
        p3[g, d, part:] += rb1[g, 0, d].astype(F32) + rb2[g, d].astype(F32)

        @pl.when(d != 0)
        def _():
            s3[g, d] = p3[g, d].astype(BF16).reshape(s3.shape[2:])
            copy_z(g, d).start()

    def item(t):
        i = t % 4
        return t // 4, jnp.where(i < 2, i + 2, 3 - i)

    def sum_step(t, carry):
        @pl.when(t == 4)
        def _():
            finish_gram(1)

        @pl.when(t < 8)
        def _():
            first_stage(*item(t))

        @pl.when((t >= 1) & (t < 9))
        def _():
            second_stage(*item(t - 1))

        @pl.when(t >= 2)
        def _():
            third_stage(*item(t - 2))

        return carry

    lax.fori_loop(0, 10, sum_step, 0)
    for g in (0, 1):
        total = p3[g, 0]
        for d in (2, 3, 1):
            copy_z(g, d).wait_recv()
            total += r3[g, d].astype(F32).reshape(rows, half)
        basis_out[:, g * half:(g + 1) * half] = total
        gath[e, :, :, g * half:(g + 1) * half] = total.astype(BF16).reshape(2, part, half)

    def held(d, yr, xr):
        return chunk(z_of(d), yr, xr)

    def pass_on(c, part, sem, at, where):
        return remote(gath.at[c, part], gath.at[c, part], sem, at, where)

    copy_gz = lambda d: remote(gath.at[e], gath.at[e], gz_sem, (d,), to_z(d))
    copy_ga1 = lambda d: pass_on(held(d, 0, 0), 0, ga1_sem, (d,), to_y)
    copy_gb1 = lambda d: pass_on(held(d, 0, 0), 1, gb1_sem, (d,), to_x)
    copy_ga2 = lambda yr, d: pass_on(held(d, yr, 0), 0, ga2_sem, (yr, d), to_x)
    copy_gb2 = lambda xr, d: pass_on(held(d, 0, xr), 1, gb2_sem, (xr, d), to_y)

    def came_z(d):
        c = held(d, 0, 0)
        return remote(gath.at[c], gath.at[c], gz_sem, (d,), to_z(d))

    def came_a1(d):
        return pass_on(held(d, 1, 0), 0, ga1_sem, (d,), to_y)

    def came_b1(d):
        return pass_on(held(d, 0, 1), 1, gb1_sem, (d,), to_x)

    def came_a2(yr, d):
        return pass_on(held(d, yr, 1), 0, ga2_sem, (yr, d), to_x)

    def came_b2(xr, d):
        return pass_on(held(d, 1, xr), 1, gb2_sem, (xr, d), to_y)

    copy_gz(1).start()
    copy_gz(2).start()
    coef[...] = jnp.zeros_like(coef)

    def add_coef(c):
        block = gath[c].reshape(rows, gath.shape[3])
        value = contract0(block, w_rows(c))
        width = value.shape[1] // 2
        coef[0] += value[:, :width]
        coef[1] += value[:, width:]

    def hand_out(d):
        copy_ga1(d).start()
        copy_gb1(d).start()
        copy_ga2(0, d).start()
        copy_gb2(0, d).start()

    def take_near(d):
        came_b2(0, d).wait_recv()
        came_a2(0, d).wait_recv()

    def take_far(d):
        came_a2(1, d).wait_recv()
        came_b2(1, d).wait_recv()

    def add_whole(d):
        take_near(d)
        take_far(d)
        first = z_of(d) * 4
        block = gath[pl.ds(first, 4)].reshape(4 * rows, gath.shape[3])
        value = contract0(block, w[pl.ds(pl.multiple_of(first * rows, rows), 4 * rows), :])
        width = value.shape[1] // 2
        coef[0] += value[:, :width]
        coef[1] += value[:, width:]

    def gather_step(d, carry):
        @pl.when(d >= 1)
        def _():
            came_z(d).wait_recv()

        hand_out(d)

        @pl.when(d == 1)
        def _():
            copy_gz(3).start()

        @pl.when(d >= 2)
        def _():
            add_whole(d - 2)

        came_a1(d).wait_recv()
        copy_ga2(1, d).start()
        came_b1(d).wait_recv()
        copy_gb2(1, d).start()
        return carry

    lax.fori_loop(0, 4, gather_step, 0)
    add_coef(held(3, 0, 0))
    add_whole(2)
    take_near(3)
    add_coef(held(3, 1, 0))
    add_coef(held(3, 0, 1))
    take_far(3)
    add_coef(held(3, 1, 1))

    share = remote(coef.at[1 - s], c_recv, c_sem, (), to_core)
    share.start()

    def drain(d, carry):
        for k in (0, 1):
            for g in (0, 1):
                copy_a1(g, k, d).wait_send()
                copy_b1(g, k, d).wait_send()
            copy_a2(k, d).wait_send()
            copy_b2(k, d).wait_send()
            copy_ga2(k, d).wait_send()
            copy_gb2(k, d).wait_send()
        copy_ga1(d).wait_send()
        copy_gb1(d).wait_send()
        return carry

    lax.fori_loop(0, 4, drain, 0)
    for d in (1, 2, 3):
        copy_z(0, d).wait_send()
        copy_z(1, d).wait_send()
        copy_gz(d).wait_send()
    for q in range(1, 8):
        copy_rows(0, q).wait_send()
        copy_rows(1, q).wait_send()
    for copy in (swap, across, own, hand):
        copy.wait_send()
    for g in (0, 1):
        for copy in (copy_gs(0, g), copy_gs(1, g), spread(g)):
            copy.wait_send()
    cross(1).wait_send()
    share.wait()
    coef_out[...] = coef[s] + c_recv[...]


def panel_call(weight, probe, routes, tokens, row_mean):
    depth, width = weight.shape
    cols = probe.shape[1]
    cap = routes.shape[1]
    rows, half = depth // 16, cols // 2
    part, quarter = rows // 2, half // 2
    dma = pltpu.SemaphoreType.DMA
    vmem = pltpu.VMEM
    return pl.pallas_call(
        functools.partial(panel_kernel, row_mean),
        out_shape=(
            jax.ShapeDtypeStruct((rows, cols), F32),
            jax.ShapeDtypeStruct((cols, width // 2), F32),
        ),
        in_specs=[pl.BlockSpec(memory_space=pltpu.HBM)] * 3 + [pl.BlockSpec(memory_space=vmem)],
        out_specs=[pl.BlockSpec(memory_space=vmem)] * 2,
        scratch_shapes=[
            vmem(tokens.shape, BF16),
            vmem((depth, width), BF16),
            vmem((depth, cols), BF16),
            vmem((2, 8, cap, width), BF16),
            vmem((2, 8, cap, width), BF16),
            vmem((2, half, width), F32),
            vmem((half, width), F32),
            vmem((2, 2, half, width), BF16),
            vmem((2, 2, 2, quarter, width), F32),
            vmem((2, 2, quarter, width), F32),
            vmem((2, quarter, width), BF16),
            vmem((2, quarter, width), BF16),
            vmem((2, 2, quarter, width), BF16),
            vmem((2, 2, 4, part, half), BF16),
            vmem((2, 2, 4, part, half), BF16),
            vmem((2, 2, 4, part, half), BF16),
            vmem((2, 2, 4, part, half), BF16),
            vmem((2, 4, part, half), F32),
            vmem((2, 4, part, half), F32),
            vmem((4, 2, part, half), F32),
            vmem((2, 4, rows, half), F32),
            vmem((2, 4, part, half), BF16),
            vmem((2, 4, part, half), BF16),
            vmem((2, 4, part, half), BF16),
            vmem((2, 4, part, half), BF16),
            vmem((2, 4, 2, part, half), BF16),
            vmem((2, 4, 2, part, half), BF16),
            vmem((16, 2, part, cols), BF16),
            vmem((2, cols, width // 2), F32),
            vmem((cols, width // 2), F32),
            dma((3,)),
            dma((2, 2, 8)),
            dma((2,)),
            dma((2,)),
            dma((2,)),
            dma((2,)),
            dma((2, 2, 2)),
            dma((2, 2)),
            dma((2, 2)),
            dma((2, 2, 2, 4)),
            dma((2, 2, 2, 4)),
            dma((2, 2, 4)),
            dma((2, 2, 4)),
            dma((2, 2, 4)),
            dma((2, 4)),
            dma((2, 4)),
            dma((2, 4)),
            dma((2, 2, 4)),
            dma((2, 2, 4)),
            dma((2,)),
        ],
        compiler_params=pltpu.CompilerParams(
            collective_id=0, has_side_effects=True, vmem_limit_bytes=52 * 2**20
        ),
        cost_estimate=pl.CostEstimate(
            flops=8 * depth * width * cols, bytes_accessed=2 * depth * width, transcendentals=0
        ),
    )(weight, probe, tokens, routes)


def body(hidden_rows, routes, down_weight, probe):
    weight = down_weight[0]
    tok_count, top_count = routes.shape
    feature_width = hidden_rows.shape[2]
    experts = lax.axis_size("expert")
    capacity = 2 * tok_count * top_count // experts
    row_mean = tok_count * top_count * lax.axis_size("seq")
    if experts == 16 and lax.axis_size("seq") == 2:
        tokens = hidden_rows.reshape(-1, feature_width)
        basis_rows, coefficients = panel_call(weight, probe, routes.T, tokens, row_mean)
        return (basis_rows, coefficients[None])
    partial_value = lax.dot_general(
        weight, probe, (((0,), (0,)), ((), ())), preferred_element_type=jnp.float32
    )
    probe_proj = lax.psum(partial_value, "seq").astype(jnp.bfloat16)
    expert_ids = routes.reshape(-1)
    onehot = (expert_ids[:, None] == jnp.arange(experts, dtype=jnp.int32)[None, :]).astype(
        jnp.int32
    )
    position = jnp.sum(onehot * (jnp.cumsum(onehot, axis=0) - 1), axis=1)
    destination = expert_ids * capacity + position
    outgoing = jnp.zeros((experts * capacity, feature_width), jnp.bfloat16)
    outgoing = outgoing.at[destination].set(hidden_rows.reshape(-1, feature_width))
    outgoing = outgoing.reshape(experts, capacity, feature_width)
    arrived = lax.all_to_all(outgoing, "expert", split_axis=0, concat_axis=0, tiled=True)
    arrived_rows = arrived.reshape(-1, feature_width)
    mixed = jnp.dot(arrived_rows, probe_proj, preferred_element_type=jnp.float32).astype(
        jnp.bfloat16
    )
    gram_part = lax.dot_general(
        arrived_rows, mixed, (((0,), (0,)), ((), ())), preferred_element_type=jnp.float32
    )
    gram_full = lax.psum(gram_part, "seq") / row_mean
    panel_image = jnp.dot(
        weight, gram_full.astype(jnp.bfloat16), preferred_element_type=jnp.float32
    )
    basis_rows = lax.psum_scatter(panel_image, "expert", scatter_dimension=0, tiled=True)
    coef_part = lax.dot_general(
        lax.all_gather(basis_rows.astype(jnp.bfloat16), "expert", axis=0, tiled=True),
        weight,
        (((0,), (0,)), ((), ())),
        preferred_element_type=jnp.float32,
    )
    coefficients = lax.psum_scatter(coef_part, "seq", scatter_dimension=1, tiled=True)
    return (basis_rows, coefficients[None])


def solution(mesh):
    in_specs = (
        P(("expert", "seq"), None, None),
        P(("expert", "seq"), None),
        P("expert", "seq", None),
        P("seq", None),
    )
    out_specs = (P(("seq", "expert"), None), P("expert", None, "seq"))
    return jax.shard_map(body, mesh=mesh, in_specs=in_specs, out_specs=out_specs, check_vma=False)
```

```python
import functools

import jax
import jax.numpy as jnp
from jax import lax
from jax.experimental import pallas as pl
from jax.experimental.pallas import tpu as pltpu
from jax.sharding import PartitionSpec as P

MESH = pl.DeviceIdType.MESH
F32 = jnp.float32
BF16 = jnp.bfloat16


def contract0(a, b):
    return lax.dot_general(a, b, (((0,), (0,)), ((), ())), preferred_element_type=F32)


def contract1(a, b):
    return lax.dot_general(a, b, (((1,), (1,)), ((), ())), preferred_element_type=F32)


def panel_kernel(
    row_mean, w_any, probe_any, tokens_any, routes, basis_out, coef_out,
    tokens, w, probe, sent, arr, p_part, p_recv, pt, gt, gr, sp, rp, g_bf, sa1, sb1, ra1, rb1, pa2, pb2, whole, p3, sa2, sb2, ra2, rb2, s3, r3, gath, coef, c_recv,
    load_sem, rows_sem, p_sem, px_sem, po_sem, pf_sem, gs_sem, gx_sem, gf_sem, a1_sem, b1_sem, a2_sem, b2_sem, z_sem, gz_sem, ga1_sem, gb1_sem, ga2_sem, gb2_sem, c_sem,
):
    e, s = lax.axis_index("expert"), lax.axis_index("seq")
    x, y, z = e % 2, (e // 2) % 2, e // 4
    to_x = {"expert": e + 1 - 2 * x}
    to_y = {"expert": e + 2 - 4 * y}
    to_core = {"seq": 1 - s}

    def z_of(k):
        return (z // 2 + k // 2) % 2 * 2 + (z + k) % 2

    def to_z(k):
        return {"expert": z_of(k) * 4 + e % 4}

    rows, half = basis_out.shape[0], basis_out.shape[1] // 2

    def chunk(zz, yr, xr):
        return zz * 4 + ((y + yr) % 2) * 2 + (x + xr) % 2

    def w_rows(c):
        return w[pl.ds(pl.multiple_of(c * rows, rows), rows), :]

    def remote(src, dst, sem, at, where):
        return pltpu.make_async_remote_copy(
            src_ref=src, dst_ref=dst, send_sem=sem.at[(0, *at)], recv_sem=sem.at[(1, *at)],
            device_id=where, device_id_type=MESH,
        )

    top, cap = routes.shape
    own_half = z // 2
    partner = {"expert": (e + 8) % 16}

    def near_chip(q):
        return own_half * 8 + (z + q // 4) % 2 * 4 + (y + q // 2) % 2 * 2 + (x + q) % 2

    load_w = pltpu.make_async_copy(w_any, w, load_sem.at[0])
    load_probe = pltpu.make_async_copy(probe_any, probe, load_sem.at[1])
    load_tokens = pltpu.make_async_copy(tokens_any, tokens, load_sem.at[2])
    load_tokens.start()
    load_w.start()
    load_probe.start()

    barrier = pltpu.get_barrier_semaphore()
    for q in range(1, 8):
        pl.semaphore_signal(
            barrier, inc=1, device_id={"expert": near_chip(q)}, device_id_type=MESH
        )
    far = [{"expert": (2 - 2 * own_half + k) * 4 + e % 4} for k in (0, 1)]
    for where in (to_core, *far):
        pl.semaphore_signal(barrier, inc=1, device_id=where, device_id_type=MESH)

    amount = tokens.shape[0]
    lane = lax.broadcasted_iota(jnp.int32, (cap, amount), 1)
    token = lax.broadcasted_iota(jnp.int32, (cap, amount), 0)
    inside = lane - token * top
    widen = jnp.where((inside >= 0) & (inside < top), 1.0, 0.0).astype(BF16)
    wide = jnp.dot(routes[...].astype(F32).astype(BF16), widen, preferred_element_type=F32)
    turn_at = lax.rem(lax.broadcasted_iota(jnp.int32, (top, amount), 1), top)
    line_at = lax.broadcasted_iota(jnp.int32, (top, amount), 0)
    names = jnp.sum(jnp.where(turn_at == line_at, wide, 0.0), axis=0, keepdims=True).astype(jnp.int32)
    mark = (lax.broadcasted_iota(jnp.int32, (16, amount), 0) == names).astype(F32)
    before = (
        lax.broadcasted_iota(jnp.int32, (amount, amount), 0)
        < lax.broadcasted_iota(jnp.int32, (amount, amount), 1)
    ).astype(F32).astype(BF16)
    rank = jnp.dot(mark.astype(BF16), before, preferred_element_type=F32)
    place = jnp.sum(mark * rank, axis=0, keepdims=True).astype(jnp.int32) + names * cap

    def slot_chip(i):
        return near_chip(5 * i % 8)

    copy_rows = lambda k, i: remote(
        sent.at[k, i], arr.at[k, i], rows_sem, (k, i), {"expert": slot_chip(i)}
    )

    def blocks_for(slots):
        line = lax.broadcasted_iota(jnp.int32, (2 * cap, amount), 0)
        picks = []
        for i in slots:
            chip = slot_chip(i)
            wanted = jnp.where(line < cap, chip * cap + line, ((chip + 8) % 16 - 1) * cap + line)
            picks.append((wanted == place).astype(F32).astype(BF16))
        pick = jnp.concatenate(picks, axis=0)
        found = jnp.dot(pick, tokens[...], preferred_element_type=F32).astype(BF16)
        return found.reshape(len(slots), 2, cap, found.shape[1])

    load_tokens.wait()
    pl.semaphore_wait(barrier, 10)

    def send_rows(i, block):
        for k in (0, 1):
            sent[k, i] = block[k]
            copy_rows(k, i).start()

    def send_pair(j, carry):
        i = 2 * j + 1
        blocks = blocks_for((i, i + 1))
        send_rows(i, blocks[0])
        send_rows(i + 1, blocks[1])
        return carry

    lax.fori_loop(0, 3, send_pair, 0)
    blocks = blocks_for((7, 0))
    send_rows(7, blocks[0])
    arr[0, 0] = blocks[1, 0]
    arr[1, 0] = blocks[1, 1]

    load_probe.wait()
    load_w.wait()
    p_part[...] = jnp.zeros_like(p_part)
    part = 512

    def project(i, carry):
        at = pl.ds(pl.multiple_of(i * part, part), part)
        p_part[...] += contract0(probe[at, :], w[at, :]).reshape(p_part.shape)
        return carry

    lax.fori_loop(0, w.shape[0] // part, project, 0)
    swap = remote(p_part.at[1 - s], p_recv, p_sem, (), to_core)
    swap.start()
    swap.wait_recv()
    pt[0, s] = (p_part[s] + p_recv[...]).astype(BF16)
    across = remote(pt.at[0, s], pt.at[1, s], px_sem, (), partner)
    across.start()
    own = remote(pt.at[0, s], pt.at[0, s], po_sem, (), to_core)
    own.start()
    remote(pt.at[0, 1 - s], pt.at[0, 1 - s], po_sem, (), to_core).wait_recv()

    def gram_of(k, first):
        rows_k = arr[k, first:first + 4].reshape(4 * cap, arr.shape[3])
        proj = pt[k].reshape(2 * pt.shape[2], pt.shape[3])
        mixed = contract1(rows_k, proj).astype(BF16)
        return contract0(mixed, rows_k).reshape(gt.shape[1:])

    for q in (1, 2, 3):
        copy_rows(0, q).wait_recv()
    gt[0] = gram_of(0, 0)
    across.wait_recv()
    hand = remote(pt.at[1, s], pt.at[1, s], pf_sem, (), to_core)
    hand.start()
    for q in (1, 2, 3):
        copy_rows(1, q).wait_recv()
    remote(pt.at[1, 1 - s], pt.at[1, 1 - s], pf_sem, (), to_core).wait_recv()
    gt[1] = gram_of(1, 0)
    for q in (4, 5, 6, 7):
        copy_rows(1, q).wait_recv()
    gt[1] += gram_of(1, 4)
    copy_gs = lambda k, g: remote(gt.at[k, g, 1 - s], gr.at[k, g], gs_sem, (k, g), to_core)
    cross = lambda g: remote(sp.at[g], rp.at[g], gx_sem, (g,), partner)
    spread = lambda g: remote(g_bf.at[g, s], g_bf.at[g, s], gf_sem, (g,), to_core)
    for g in (0, 1):
        copy_gs(1, g).start()
    copy_gs(1, 0).wait_recv()
    sp[0] = (gt[1, 0, s] + gr[1, 0]).astype(BF16)
    cross(0).start()
    for q in (4, 5, 6, 7):
        copy_rows(0, q).wait_recv()
    gt[0] += gram_of(0, 4)
    for g in (0, 1):
        copy_gs(0, g).start()

    def finish_gram(g):
        copy_gs(0, g).wait_recv()
        cross(g).wait_recv()
        total = gt[0, g, s] + gr[0, g] + rp[g].astype(F32)
        g_bf[g, s] = (total / row_mean).astype(BF16)
        spread(g).start()
        remote(g_bf.at[g, 1 - s], g_bf.at[g, 1 - s], gf_sem, (g,), to_core).wait_recv()

    copy_gs(1, 1).wait_recv()
    sp[1] = (gt[1, 1, s] + gr[1, 1]).astype(BF16)
    cross(0).wait_send()
    cross(1).start()
    finish_gram(0)

    part = rows // 2

    copy_a1 = lambda g, yr, d: remote(sa1.at[g, yr, d], ra1.at[g, yr, d], a1_sem, (g, yr, d), to_x)
    copy_b1 = lambda g, xr, d: remote(sb1.at[g, xr, d], rb1.at[g, xr, d], b1_sem, (g, xr, d), to_y)
    copy_a2 = lambda g, d: remote(sa2.at[g, d], ra2.at[g, d], a2_sem, (g, d), to_y)
    copy_b2 = lambda g, d: remote(sb2.at[g, d], rb2.at[g, d], b2_sem, (g, d), to_x)
    copy_z = lambda g, d: remote(s3.at[g, d], r3.at[g, d], z_sem, (g, d), to_z(d))

    def first_stage(g, d):
        at = pl.ds(pl.multiple_of(z_of(d) * 4 * rows, rows), 4 * rows)
        value = contract1(w[at, :], g_bf[g].reshape(half, g_bf.shape[3]))
        whole[...] = value.reshape(whole.shape)
        place_of = lambda yr, xr: (y + yr) % 2 * 2 + (x + xr) % 2
        c = place_of(1, 1)
        sa1[g, 1, d] = whole[c, 0].astype(BF16)
        copy_a1(g, 1, d).start()
        sb1[g, 1, d] = whole[c, 1].astype(BF16)
        copy_b1(g, 1, d).start()
        c = place_of(0, 1)
        sa1[g, 0, d] = whole[c, 0].astype(BF16)
        copy_a1(g, 0, d).start()
        pb2[g, d] = whole[c, 1]
        c = place_of(1, 0)
        sb1[g, 0, d] = whole[c, 1].astype(BF16)
        copy_b1(g, 0, d).start()
        pa2[g, d] = whole[c, 0]
        p3[g, d] = whole[place_of(0, 0)].reshape(rows, half)

    def second_stage(g, d):
        copy_a1(g, 1, d).wait_recv()
        sa2[g, d] = (pa2[g, d] + ra1[g, 1, d].astype(F32)).astype(BF16)
        copy_a2(g, d).start()
        copy_b1(g, 1, d).wait_recv()
        sb2[g, d] = (pb2[g, d] + rb1[g, 1, d].astype(F32)).astype(BF16)
        copy_b2(g, d).start()

    def third_stage(g, d):
        copy_a1(g, 0, d).wait_recv()
        copy_a2(g, d).wait_recv()
        p3[g, d, :part] += ra1[g, 0, d].astype(F32) + ra2[g, d].astype(F32)
        copy_b1(g, 0, d).wait_recv()
        copy_b2(g, d).wait_recv()
        p3[g, d, part:] += rb1[g, 0, d].astype(F32) + rb2[g, d].astype(F32)

        @pl.when(d != 0)
        def _():
            s3[g, d] = p3[g, d].astype(BF16).reshape(s3.shape[2:])
            copy_z(g, d).start()

    def item(t):
        i = t % 4
        return t // 4, jnp.where(i < 2, i + 2, 3 - i)

    def sum_step(t, carry):
        @pl.when((t >= 2) & (t < 10))
        def _():
            second_stage(*item(t - 2))

        @pl.when(t == 4)
        def _():
            finish_gram(1)

        @pl.when(t < 8)
        def _():
            first_stage(*item(t))

        @pl.when(t >= 4)
        def _():
            third_stage(*item(t - 4))

        return carry

    lax.fori_loop(0, 12, sum_step, 0)
    for g in (0, 1):
        total = p3[g, 0]
        for d in (2, 3, 1):
            copy_z(g, d).wait_recv()
            total += r3[g, d].astype(F32).reshape(rows, half)
        basis_out[:, g * half:(g + 1) * half] = total
        gath[e, :, :, g * half:(g + 1) * half] = total.astype(BF16).reshape(2, part, half)

    def held(d, yr, xr):
        return chunk(z_of(d), yr, xr)

    def pass_on(c, part, sem, at, where):
        return remote(gath.at[c, part], gath.at[c, part], sem, at, where)

    copy_gz = lambda d: remote(gath.at[e], gath.at[e], gz_sem, (d,), to_z(d))
    copy_ga1 = lambda d: pass_on(held(d, 0, 0), 0, ga1_sem, (d,), to_y)
    copy_gb1 = lambda d: pass_on(held(d, 0, 0), 1, gb1_sem, (d,), to_x)
    copy_ga2 = lambda yr, d: pass_on(held(d, yr, 0), 0, ga2_sem, (yr, d), to_x)
    copy_gb2 = lambda xr, d: pass_on(held(d, 0, xr), 1, gb2_sem, (xr, d), to_y)

    def came_z(d):
        c = held(d, 0, 0)
        return remote(gath.at[c], gath.at[c], gz_sem, (d,), to_z(d))

    def came_a1(d):
        return pass_on(held(d, 1, 0), 0, ga1_sem, (d,), to_y)

    def came_b1(d):
        return pass_on(held(d, 0, 1), 1, gb1_sem, (d,), to_x)

    def came_a2(yr, d):
        return pass_on(held(d, yr, 1), 0, ga2_sem, (yr, d), to_x)

    def came_b2(xr, d):
        return pass_on(held(d, 1, xr), 1, gb2_sem, (xr, d), to_y)

    copy_gz(1).start()
    copy_gz(2).start()
    coef[...] = jnp.zeros_like(coef)

    def add_coef(c):
        block = gath[c].reshape(rows, gath.shape[3])
        value = contract0(block, w_rows(c))
        width = value.shape[1] // 2
        coef[0] += value[:, :width]
        coef[1] += value[:, width:]

    def hand_out(d):
        copy_ga1(d).start()
        copy_gb1(d).start()
        copy_ga2(0, d).start()
        copy_gb2(0, d).start()

    def take_near(d):
        came_b2(0, d).wait_recv()
        came_a2(0, d).wait_recv()

    def take_far(d):
        came_a2(1, d).wait_recv()
        came_b2(1, d).wait_recv()

    def add_whole(d):
        take_near(d)
        take_far(d)
        first = z_of(d) * 4
        block = gath[pl.ds(first, 4)].reshape(4 * rows, gath.shape[3])
        value = contract0(block, w[pl.ds(pl.multiple_of(first * rows, rows), 4 * rows), :])
        width = value.shape[1] // 2
        coef[0] += value[:, :width]
        coef[1] += value[:, width:]

    def gather_step(d, carry):
        @pl.when(d >= 1)
        def _():
            came_z(d).wait_recv()

        hand_out(d)

        @pl.when(d == 1)
        def _():
            copy_gz(3).start()

        @pl.when(d >= 2)
        def _():
            add_whole(d - 2)

        came_a1(d).wait_recv()
        copy_ga2(1, d).start()
        came_b1(d).wait_recv()
        copy_gb2(1, d).start()
        return carry

    lax.fori_loop(0, 4, gather_step, 0)
    add_coef(held(3, 0, 0))
    add_whole(2)
    take_near(3)
    add_coef(held(3, 1, 0))
    add_coef(held(3, 0, 1))
    take_far(3)
    add_coef(held(3, 1, 1))

    share = remote(coef.at[1 - s], c_recv, c_sem, (), to_core)
    share.start()

    def drain(d, carry):
        for k in (0, 1):
            for g in (0, 1):
                copy_a1(g, k, d).wait_send()
                copy_b1(g, k, d).wait_send()
            copy_a2(k, d).wait_send()
            copy_b2(k, d).wait_send()
            copy_ga2(k, d).wait_send()
            copy_gb2(k, d).wait_send()
        copy_ga1(d).wait_send()
        copy_gb1(d).wait_send()
        return carry

    lax.fori_loop(0, 4, drain, 0)
    for d in (1, 2, 3):
        copy_z(0, d).wait_send()
        copy_z(1, d).wait_send()
        copy_gz(d).wait_send()
    for q in range(1, 8):
        copy_rows(0, q).wait_send()
        copy_rows(1, q).wait_send()
    for copy in (swap, across, own, hand):
        copy.wait_send()
    for g in (0, 1):
        for copy in (copy_gs(0, g), copy_gs(1, g), spread(g)):
            copy.wait_send()
    cross(1).wait_send()
    share.wait()
    coef_out[...] = coef[s] + c_recv[...]


def panel_call(weight, probe, routes, tokens, row_mean):
    depth, width = weight.shape
    cols = probe.shape[1]
    cap = routes.shape[1]
    rows, half = depth // 16, cols // 2
    part, quarter = rows // 2, half // 2
    dma = pltpu.SemaphoreType.DMA
    vmem = pltpu.VMEM
    return pl.pallas_call(
        functools.partial(panel_kernel, row_mean),
        out_shape=(
            jax.ShapeDtypeStruct((rows, cols), F32),
            jax.ShapeDtypeStruct((cols, width // 2), F32),
        ),
        in_specs=[pl.BlockSpec(memory_space=pltpu.HBM)] * 3 + [pl.BlockSpec(memory_space=vmem)],
        out_specs=[pl.BlockSpec(memory_space=vmem)] * 2,
        scratch_shapes=[
            vmem(tokens.shape, BF16),
            vmem((depth, width), BF16),
            vmem((depth, cols), BF16),
            vmem((2, 8, cap, width), BF16),
            vmem((2, 8, cap, width), BF16),
            vmem((2, half, width), F32),
            vmem((half, width), F32),
            vmem((2, 2, half, width), BF16),
            vmem((2, 2, 2, quarter, width), F32),
            vmem((2, 2, quarter, width), F32),
            vmem((2, quarter, width), BF16),
            vmem((2, quarter, width), BF16),
            vmem((2, 2, quarter, width), BF16),
            vmem((2, 2, 4, part, half), BF16),
            vmem((2, 2, 4, part, half), BF16),
            vmem((2, 2, 4, part, half), BF16),
            vmem((2, 2, 4, part, half), BF16),
            vmem((2, 4, part, half), F32),
            vmem((2, 4, part, half), F32),
            vmem((4, 2, part, half), F32),
            vmem((2, 4, rows, half), F32),
            vmem((2, 4, part, half), BF16),
            vmem((2, 4, part, half), BF16),
            vmem((2, 4, part, half), BF16),
            vmem((2, 4, part, half), BF16),
            vmem((2, 4, 2, part, half), BF16),
            vmem((2, 4, 2, part, half), BF16),
            vmem((16, 2, part, cols), BF16),
            vmem((2, cols, width // 2), F32),
            vmem((cols, width // 2), F32),
            dma((3,)),
            dma((2, 2, 8)),
            dma((2,)),
            dma((2,)),
            dma((2,)),
            dma((2,)),
            dma((2, 2, 2)),
            dma((2, 2)),
            dma((2, 2)),
            dma((2, 2, 2, 4)),
            dma((2, 2, 2, 4)),
            dma((2, 2, 4)),
            dma((2, 2, 4)),
            dma((2, 2, 4)),
            dma((2, 4)),
            dma((2, 4)),
            dma((2, 4)),
            dma((2, 2, 4)),
            dma((2, 2, 4)),
            dma((2,)),
        ],
        compiler_params=pltpu.CompilerParams(
            collective_id=0, has_side_effects=True, vmem_limit_bytes=61072 * 2**10
        ),
        cost_estimate=pl.CostEstimate(
            flops=8 * depth * width * cols, bytes_accessed=2 * depth * width, transcendentals=0
        ),
    )(weight, probe, tokens, routes)


def body(hidden_rows, routes, down_weight, probe):
    weight = down_weight[0]
    tok_count, top_count = routes.shape
    feature_width = hidden_rows.shape[2]
    experts = lax.axis_size("expert")
    capacity = 2 * tok_count * top_count // experts
    row_mean = tok_count * top_count * lax.axis_size("seq")
    if experts == 16 and lax.axis_size("seq") == 2:
        tokens = hidden_rows.reshape(-1, feature_width)
        basis_rows, coefficients = panel_call(weight, probe, routes.T, tokens, row_mean)
        return (basis_rows, coefficients[None])
    partial_value = lax.dot_general(
        weight, probe, (((0,), (0,)), ((), ())), preferred_element_type=jnp.float32
    )
    probe_proj = lax.psum(partial_value, "seq").astype(jnp.bfloat16)
    expert_ids = routes.reshape(-1)
    onehot = (expert_ids[:, None] == jnp.arange(experts, dtype=jnp.int32)[None, :]).astype(
        jnp.int32
    )
    position = jnp.sum(onehot * (jnp.cumsum(onehot, axis=0) - 1), axis=1)
    destination = expert_ids * capacity + position
    outgoing = jnp.zeros((experts * capacity, feature_width), jnp.bfloat16)
    outgoing = outgoing.at[destination].set(hidden_rows.reshape(-1, feature_width))
    outgoing = outgoing.reshape(experts, capacity, feature_width)
    arrived = lax.all_to_all(outgoing, "expert", split_axis=0, concat_axis=0, tiled=True)
    arrived_rows = arrived.reshape(-1, feature_width)
    mixed = jnp.dot(arrived_rows, probe_proj, preferred_element_type=jnp.float32).astype(
        jnp.bfloat16
    )
    gram_part = lax.dot_general(
        arrived_rows, mixed, (((0,), (0,)), ((), ())), preferred_element_type=jnp.float32
    )
    gram_full = lax.psum(gram_part, "seq") / row_mean
    panel_image = jnp.dot(
        weight, gram_full.astype(jnp.bfloat16), preferred_element_type=jnp.float32
    )
    basis_rows = lax.psum_scatter(panel_image, "expert", scatter_dimension=0, tiled=True)
    coef_part = lax.dot_general(
        lax.all_gather(basis_rows.astype(jnp.bfloat16), "expert", axis=0, tiled=True),
        weight,
        (((0,), (0,)), ((), ())),
        preferred_element_type=jnp.float32,
    )
    coefficients = lax.psum_scatter(coef_part, "seq", scatter_dimension=1, tiled=True)
    return (basis_rows, coefficients[None])


def solution(mesh):
    in_specs = (
        P(("expert", "seq"), None, None),
        P(("expert", "seq"), None),
        P("expert", "seq", None),
        P("seq", None),
    )
    out_specs = (P(("seq", "expert"), None), P("expert", None, "seq"))
    return jax.shard_map(body, mesh=mesh, in_specs=in_specs, out_specs=out_specs, check_vma=False)
```
